256 devices in a mesh: ka: 16 (over x_hi, z), pt: 16 (over y, x_lo, core).
Axes of the slice: x: 4 (x_hi: 2, x_lo: 2; x = x_hi * 2 + x_lo), y: 4, z: 8, core: 2. Of those that a mesh axis runs over, the one named last changes fastest.
Arguments:
- wedge_orbitals: bfloat16 [2, 16, 4096, 128], P(None, 'ka', 'pt'), may hold values from -6 to 6
- star_members: int32 [16, 4], replicated, may hold values from -1 to 15, as said below
- star_ops: int32 [16, 4], replicated, may hold values from 0 to 47
- rotations: bfloat16 [48, 128, 128], replicated, may hold values from -0.5 to 0.5
- screen_left: bfloat16 [6, 4096, 64], P(None, 'pt'), may hold values from -2.5 to 2.5
- screen_right: bfloat16 [6, 4096, 64], P(None, 'pt'), may hold values from -2.5 to 2.5
Outputs:
- exchange_matrix: float32 [2, 16, 128, 128], P(None, 'ka', 'pt')
The draws below stay inside these ranges and needn't reach their ends.
Inputs may be any that keep to these rules, and one draw needn't show every extreme that they name: `star_members`: every k-point 0 to 15 stands exactly once in the table; -1 marks an empty slot; the star of some wedge point fills all 4 slots.
All inputs are finite; a program needn't handle non-finite values.
Results may differ from the reference program's by a relative error of at most 0.0064.
Values may be sent and summed in bfloat16 or wider, within the bound.
A program may use at most 64 MiB of HBM per device.

```python
import math
import jax
import jax.numpy as jnp
from jax import lax

NB = 128
NPTS = 4096
RANK = 64
NOPS = 48
MULT = 4
STOPS = 6
QBLK = 1024
NK = 16
NW = 16


def draw_star_members(key, part):
    n_slots = NW * MULT
    key_row = jax.random.fold_in(key, 11)
    key_slots = jax.random.fold_in(key, 12)
    key_kpts = jax.random.fold_in(key, 13)
    full_row = jax.random.randint(key_row, (), 0, NW)
    slot_order = jax.random.permutation(key_slots, n_slots).astype(jnp.int32)
    row_of = slot_order // MULT
    scores = jnp.where(row_of == full_row, 0, 1).astype(jnp.int32) * n_slots + jnp.arange(n_slots, dtype=jnp.int32)
    ranking = jnp.argsort(scores, stable=True)
    chosen = slot_order[ranking][:NK]
    kpoint_order = jax.random.permutation(key_kpts, NK).astype(jnp.int32)
    table = jnp.full((n_slots,), -1, jnp.int32).at[chosen].set(kpoint_order)
    return table.reshape(NW, MULT)


def set_ends(values, rng, low, high):
    place = [jax.random.randint(jax.random.fold_in(rng, axis), (), 0, length) for axis, length in enumerate(values.shape)]
    main_axis = values.shape.index(max(values.shape))
    next_to = place[:main_axis] + [(place[main_axis] + 1) % values.shape[main_axis]] + place[main_axis + 1:]
    return values.at[tuple(place)].set(low).at[tuple(next_to)].set(high)


def steps_of(own_key, shape, split, least, high):
    factor_of = 1.0
    for dim, parts in split:
        steps = jax.random.uniform(jax.random.fold_in(jax.random.fold_in(own_key, 6), dim), (parts,), jnp.float32, least / len(split), high / len(split))
        factor_of = factor_of * jnp.repeat(jnp.exp(steps), shape[dim] // parts).reshape((-1,) + (1,) * (len(shape) - 1 - dim))
    return factor_of


def noise(rng, shape, deviation, limit, pieces=(), kind=jnp.bfloat16):
    gain = steps_of(rng, shape, pieces, -0.22, 0.18) if pieces else 1.0
    result = jax.random.normal(rng, shape, jnp.float32) * deviation * gain
    return jnp.minimum(jnp.maximum(result, -limit), limit).astype(kind)


def setup_inputs(seed: int = 0) -> dict:
    splits = jax.random.split(jax.random.key(seed), 7)
    return {
        "wedge_orbitals": noise(splits[0], (2, NW, NPTS, NB), 1.0, 6.0, ((1, 16), (2, 16))),
        "star_members": draw_star_members(jax.random.fold_in(splits[6], 71), 0),
        "star_ops": set_ends(jax.random.randint(splits[2], (NW, MULT), 0, NOPS), jax.random.fold_in(splits[2], 1), 0, NOPS - 1).astype(jnp.int32),
        "rotations": noise(splits[3], (NOPS, NB, NB), NB ** -0.5, 0.5),
        "screen_left": noise(splits[4], (STOPS, NPTS, RANK), 0.35, 2.5, ((1, 16),)),
        "screen_right": noise(splits[5], (STOPS, NPTS, RANK), 0.35, 2.5, ((1, 16),)),
    }


def rotated_blocks(wedge_orbitals, star_members, star_ops, rotations):
    wedge_iota = jnp.arange(NW, dtype=jnp.int32)[:, None]

    def per_kpoint(kpoint):
        located = star_members == kpoint
        wedge_index = jnp.sum(jnp.where(located, wedge_iota, 0)).astype(jnp.int32)
        op_index = jnp.sum(jnp.where(located, star_ops, 0)).astype(jnp.int32)
        arrived = lax.dynamic_index_in_dim(wedge_orbitals, wedge_index, 1, keepdims=False)
        rotation = lax.dynamic_index_in_dim(rotations, op_index, 0, keepdims=False)
        product = jnp.dot(arrived.reshape(2 * NPTS, NB), rotation, preferred_element_type=jnp.float32)
        return product.astype(jnp.bfloat16).reshape(2, NPTS, NB)
    return lax.map(per_kpoint, jnp.arange(NK, dtype=jnp.int32))

def density_term(row_block, full_block, upper_half, lower_half, left_screen, right_screen):
    n_rows = row_block.shape[1]
    left_rows = jnp.concatenate([row_block[0], row_block[1]], axis=1)
    swapped = jnp.concatenate([row_block[1], -row_block[0]], axis=1)
    stacked = jnp.concatenate([left_rows, swapped], axis=0)
    accum = jnp.zeros((n_rows, 2 * NB), jnp.float32)
    for column_block in range(NPTS // QBLK):
        col_start = column_block * QBLK
        col_end = col_start + QBLK
        column_rows = jnp.concatenate([full_block[0, col_start:col_end], full_block[1, col_start:col_end]], axis=1)
        density = lax.dot_general(stacked, column_rows, (((1,), (1,)), ((), ())), preferred_element_type=jnp.float32)
        screen_tile = lax.dot_general(left_screen, right_screen[col_start:col_end], (((1,), (1,)), ((), ())), preferred_element_type=jnp.float32)
        real_part = (density[:n_rows] * screen_tile).astype(jnp.bfloat16)
        imag_part = (density[n_rows:] * screen_tile).astype(jnp.bfloat16)
        screened = jnp.concatenate([real_part, imag_part], axis=1)
        operand = jnp.concatenate([upper_half[col_start:col_end], lower_half[col_start:col_end]], axis=0)
        accum = accum + jnp.dot(screened, operand, preferred_element_type=jnp.float32)
    return accum

def reference(wedge_orbitals, star_members, star_ops, rotations, screen_left, screen_right):
    blocks = rotated_blocks(wedge_orbitals, star_members, star_ops, rotations)
    lead_stops = STOPS // 2
    scale_factor = 1.0 / (4.0 * NPTS * math.sqrt(NB))

    def per_kpoint(kpoint):
        own_block = lax.dynamic_index_in_dim(blocks, kpoint, 0, keepdims=False)
        upper_half = jnp.concatenate([own_block[0], own_block[1]], axis=1)
        lower_half = jnp.concatenate([-own_block[1], own_block[0]], axis=1)
        accum = jnp.zeros((NPTS, 2 * NB), jnp.float32)
        for stop in range(STOPS):
            other = ((kpoint + lead_stops - stop) % NK).astype(jnp.int32)
            visited = lax.dynamic_index_in_dim(blocks, other, 0, keepdims=False)
            accum = accum + density_term(visited, visited, upper_half, lower_half, screen_left[stop], screen_right[stop])
        rounded_y = accum.astype(jnp.bfloat16)
        y_real = rounded_y[:, :NB]
        y_imag = rounded_y[:, NB:]
        stacked_x = jnp.concatenate([own_block[0], own_block[1]], axis=0)
        right_stack = jnp.concatenate([rounded_y, jnp.concatenate([y_imag, -y_real], axis=1)], axis=0)
        partial_value = lax.dot_general(stacked_x, right_stack, (((0,), (0,)), ((), ())), preferred_element_type=jnp.float32)
        partial_value = partial_value * scale_factor
        return jnp.stack([partial_value[:, :NB], partial_value[:, NB:]])
    matrices = lax.map(per_kpoint, jnp.arange(NK, dtype=jnp.int32))
    return jnp.transpose(matrices, (1, 0, 2, 3))
```

```python
import math

import jax
import jax.numpy as jnp
from jax import lax
from jax.experimental import pallas as pl
from jax.experimental.pallas import tpu as pltpu
from jax.sharding import PartitionSpec as P

NB = 128
NPTS = 4096
STOPS = 6
NK = 16
BF = jnp.bfloat16
F32 = jnp.float32
MESH = pl.DeviceIdType.MESH
RING = (0, 1, 7, 2, 6, 3, 5, 4)
GROUPS = ((0, 8, (0, 1, 7)), (8, 12, (2, 6)), (12, 18, (3, 5, 4)))


class Place:
    def __init__(self):
        ka = lax.axis_index("ka")
        pt = lax.axis_index("pt")
        self.xh = lax.div(ka, 8)
        self.z = lax.rem(ka, 8)
        self.y = lax.div(pt, 4)
        self.xl = lax.rem(lax.div(pt, 2), 2)
        self.c = lax.rem(pt, 2)
        self.x = 2 * self.xh + self.xl

    def device(self, dx=0, dy=0, dz=0, other=False):
        x = lax.rem(self.x + dx, 4)
        y = lax.rem(self.y + dy, 4)
        z = lax.rem(self.z + dz, 8)
        c = 1 - self.c if other else self.c
        return (lax.div(x, 2) * 8 + z, y * 4 + lax.rem(x, 2) * 2 + c)

    def swap(self):
        return (self.c * 8 + self.z, self.y * 4 + self.xl * 2 + self.xh)


class Copies:
    def __init__(self, send, recv):
        self.send, self.recv, self.count, self.open = send, recv, 0, []

    def make(self, src, dst, device):
        i = self.count
        self.count += 1
        return pltpu.make_async_remote_copy(
            src_ref=src,
            dst_ref=dst,
            send_sem=self.send.at[i],
            recv_sem=self.recv.at[i],
            device_id=device,
            device_id_type=MESH,
        )

    def start(self, src, dst, device):
        copy = self.make(src, dst, device)
        copy.start()
        self.open.append(copy)
        return copy

    def finish(self):
        for copy in self.open:
            copy.wait_send()


def greet(barrier, devices):
    for device in devices:
        pl.semaphore_signal(barrier, inc=1, device_id=device, device_id_type=MESH)


def stripes(place, net, qw, pw, low, high, rels, row):
    size = high - low
    half = size // 2
    slot = high - 2 * len(rels)
    for rel in rels:
        for u in range(2):
            for ri in range(2):
                qw[ri, slot, 0, 0] = pw[rel, u, ri, pl.ds(row, 16), :]
            slot += 1
    plus = (place.device(dx=1), place.device(dy=1))
    minus = (place.device(dx=3), place.device(dy=3))

    def at(h, first, second, start=low, length=size):
        tiles = pl.ds(start, length)
        if h == 0:
            return qw.at[0, tiles, second, first]
        return qw.at[1, tiles, first, second]

    def second_hop(h, arrived, firsts):
        to, fro = arrived
        to.wait_recv()
        a = net.start(at(h, firsts, 2, low, half), at(h, firsts, 3, low, half), plus[1 - h])
        fro.wait_recv()
        b = net.start(
            at(h, firsts, 1, low + half, half), at(h, firsts, 3, low + half, half), minus[1 - h]
        )
        return a, b

    def across(h, firsts):
        return (
            net.start(at(h, firsts, 0), at(h, firsts, 2), plus[1 - h]),
            net.start(at(h, firsts, 0), at(h, firsts, 1), minus[1 - h]),
        )

    one, two, own = {}, {}, {}
    for h in range(2):
        one[h] = (
            net.start(at(h, 0, 0), at(h, 2, 0), plus[h]),
            net.start(at(h, 0, 0), at(h, 1, 0), minus[h]),
        )
        own[h] = across(h, pl.ds(0, 1))
    yield
    side, last = {}, []
    for h in range(2):
        to, fro = one[h]
        to.wait_recv()
        a = net.start(at(h, 2, 0, low, half), at(h, 3, 0, low, half), plus[h])
        fro.wait_recv()
        b = net.start(
            at(h, 1, 0, low + half, half), at(h, 3, 0, low + half, half), minus[h]
        )
        two[h] = (a, b)
        side[h] = across(h, pl.ds(1, 2))
    for h in range(2):
        last.extend(second_hop(h, own[h], pl.ds(0, 1)))
    yield
    far = {}
    for h in range(2):
        for copy in two[h]:
            copy.wait_recv()
        far[h] = across(h, pl.ds(3, 1))
    for h in range(2):
        last.extend(second_hop(h, side[h], pl.ds(1, 2)))
    yield
    for h in range(2):
        last.extend(second_hop(h, far[h], pl.ds(3, 1)))
    yield
    for copy in last:
        copy.wait_recv()


def pair(ref, stop, rows):
    return jnp.concatenate([ref[stop, rows, :], ref[stop + 1, rows, :]], axis=1)


def gather(place, net, wedge, left, right, pw, qw, lp, rown):
    c, xh, z = place.c, place.xh, place.z
    straight = c == xh
    other = place.device(other=True)
    plus, minus = place.device(dz=1), place.device(dz=7)

    swap = net.make(wedge.at[:, 0], pw.at[0, xh], place.swap())

    @pl.when(c != xh)
    def _():
        swap.start()

    @pl.when(straight)
    def _():
        pw[0, c] = wedge[:, 0]

    row = pl.multiple_of(32 * z + 16 * c, 16)
    other_row = pl.multiple_of(32 * z + 16 * (1 - c), 16)
    give_left = net.make(lp, lp, other)
    give_right = net.make(rown.at[1], rown.at[0], other)

    @pl.when(straight)
    def _():
        for i in range(3):
            rown[0, i] = pair(right, 2 * i, pl.ds(row, 16))
            rown[1, i] = pair(right, 2 * i, pl.ds(other_row, 16))
        give_right.start()
        for i in range(3):
            lp[i] = pair(left, 2 * i, slice(None))
        give_left.start()

    @pl.when(c != xh)
    def _():
        swap.wait_recv()

    ups, downs, beside = {}, {}, {}

    def forward(step, ri):
        up, down = (8 - step) % 8, step
        if step < 3 or (step == 3 and ri == 0):
            ups[step, ri] = net.start(pw.at[up, c, ri], pw.at[up - 1 if up else 7, c, ri], plus)
        if step < 3 or (step == 3 and ri == 1):
            downs[step, ri] = net.start(pw.at[down, c, ri], pw.at[down + 1, c, ri], minus)

    def share(rel, ri):
        beside[rel, ri] = net.start(pw.at[rel, c, ri], pw.at[rel, c, ri], other)

    def ring(step):
        for ri in range(2):
            if step < 4:
                ups[step - 1, ri].wait_recv()
                downs[step - 1, ri].wait_recv()
                forward(step, ri)
                share(8 - step, ri)
                share(step, ri)
            else:
                (ups if ri == 0 else downs)[3, ri].wait_recv()
                share(4, ri)

    def shared(rels):
        for rel in rels:
            for ri in range(2):
                beside[rel, ri].wait_recv()

    for ri in range(2):
        forward(0, ri)
        share(0, ri)
    ring(1)

    @pl.when(c != xh)
    def _():
        give_right.wait_recv()

    for h, slot, i in ((0, 0, 0), (0, 1, 1), (1, 0, 2), (1, 1, 2)):
        qw[h, slot, 0, 0] = rown[0, i]
    flows = [stripes(place, net, qw, pw, low, high, rels, row) for low, high, rels in GROUPS]

    def advance(g):
        if g >= 0:
            next(flows[g], None)

    shared(GROUPS[0][2])
    advance(0)
    ring(2)
    advance(0)
    shared(GROUPS[1][2])
    advance(1)
    ring(3)
    advance(0)
    advance(1)
    ring(4)
    advance(0)
    shared(GROUPS[2][2])
    advance(2)
    advance(1)
    advance(0)
    advance(2)
    advance(1)
    advance(2)
    advance(1)
    advance(2)
    advance(2)

    @pl.when(c != xh)
    def _():
        give_left.wait_recv()
        swap.wait_send()

    @pl.when(straight)
    def _():
        give_right.wait_send()
        give_left.wait_send()

    net.finish()


def gather_kernel(wedge, left, right, pw, qw, lp, rown, send, recv):
    place = Place()
    net = Copies(send, recv)
    barrier = pltpu.get_barrier_semaphore()
    greet(
        barrier,
        [
            place.device(other=True),
            place.device(dx=1),
            place.device(dx=3),
            place.device(dy=1),
            place.device(dy=3),
            place.device(dz=1),
            place.device(dz=7),
        ],
    )

    @pl.when(place.c != place.xh)
    def _():
        greet(barrier, [place.swap()])
        pl.semaphore_wait(barrier, 8)

    @pl.when(place.c == place.xh)
    def _():
        pl.semaphore_wait(barrier, 7)

    gather(place, net, wedge, left, right, pw, qw, lp, rown)


def dot(a, b, ca, cb):
    return lax.dot_general(a, b, (((ca,), (cb,)), ((), ())), preferred_element_type=F32)


def tile_kernel(code, pw, qw, lp, rotations, e, wide, xp, xq, screen, density, mixed):
    z = lax.rem(lax.axis_index("ka"), 8)
    lane = lax.broadcasted_iota(jnp.int32, (256, 128), 1)
    for i, (h, slot) in enumerate(((0, 0), (0, 1), (1, 0))):
        factor = qw[h, slot].reshape(256, 128)
        rows = lp[i]
        zero = jnp.zeros_like(rows)
        screen[2 * i] = dot(jnp.where(lane < 64, rows, zero), factor, 1, 1)
        screen[2 * i + 1] = dot(jnp.where(lane < 64, zero, rows), factor, 1, 1)
    wide[...] = jnp.zeros_like(wide)

    def turn(k, carry):
        word = code[k]
        w = lax.div(word, 64)
        op = lax.rem(word, 64)
        u = lax.div(w, 8)
        rel = lax.rem(lax.rem(w, 8) - z + 8, 8)
        order = jnp.where(rel == 0, 0, jnp.where(rel <= 4, 2 * rel - 1, 16 - 2 * rel))
        slot = 2 + 2 * order + u
        rotation = rotations[op]
        b = lax.rem(k, 4)
        wide[b, :128, :128] = rotation
        wide[b, 128:, 128:] = rotation
        raw = jnp.concatenate(
            [
                jnp.concatenate([pw[rel, u, 0], pw[rel, u, 1]], axis=1),
                jnp.concatenate(
                    [qw[0, slot].reshape(256, 128), qw[1, slot].reshape(256, 128)], axis=1
                ),
            ],
            axis=0,
        )
        turned = dot(raw, wide[b], 1, 0).astype(BF)
        xp[k] = turned[:256]
        xq[k] = turned[256:]
        rows = turned[:256]
        stacked = jnp.concatenate(
            [rows, jnp.concatenate([rows[:, 128:], -rows[:, :128]], axis=1)], axis=0
        )
        density[k] = dot(stacked, turned[256:], 1, 1)
        return carry

    lax.fori_loop(0, NK, turn, 0, unroll=4)

    def mix(t, carry):
        top = pl.multiple_of(lax.rem(t, 16) * 16, 16)
        part = lax.div(t, 16)
        source = pl.multiple_of(part * 256 + top, 16)
        for lanes in (0, 128):
            cols = pl.ds(lanes, 128)
            s = [screen[i, pl.ds(top, 16), cols] for i in range(STOPS)]
            d = [density[j, pl.ds(source, 16), cols] for j in range(NK)]
            for k in range(NK):
                total = d[(k + 3) % NK] * s[0]
                for i in range(1, STOPS):
                    total = total + d[(k + 3 - i) % NK] * s[i]
                mixed[part, k, pl.ds(top, 16), cols] = total.astype(BF)
        return carry

    lax.fori_loop(0, 32, mix, 0)

    def close(k, carry):
        q = xq[k]
        operand = jnp.concatenate([-q[:, 128:], q[:, :128]], axis=1)
        y = dot(mixed[0, k], q, 1, 0) + dot(mixed[1, k], operand, 1, 0)
        y = y.astype(BF)
        rows = xp[k]
        turned = jnp.concatenate([y[:, 128:], -y[:, :128]], axis=1)
        value = dot(rows[:, :128], y, 0, 0) + dot(rows[:, 128:], turned, 0, 0)
        e[k] = value.reshape(8, 2, 8, 256)
        return carry

    lax.fori_loop(0, NK, close, 0, unroll=4)


def reduce(place, net, e, sib, sb, rb, sz, zb, out):
    c, x, y, z, xh, xl = place.c, place.x, place.y, place.z, place.xh, place.xl
    copy = net.start(e.at[:, :, 1 - c], sib, place.device(other=True))
    copy.wait_recv()
    for half in range(2):
        for g in range(8):
            for i in range(8):
                k = half * 8 + i
                value = e[k, g, c] + sib[k, g]
                value = jnp.concatenate([value[:, :128], value[:, 128:]], axis=0)
                sb[half, g, i] = value.astype(BF)
    arrivals = []
    for dx in range(4):
        for dy in range(4):
            if dx or dy:
                tx = lax.rem(x + dx, 4)
                ty = lax.rem(y + dy, 4)
                arrivals.append(
                    net.start(
                        sb.at[lax.div(tx, 2), ty * 2 + lax.rem(tx, 2)],
                        rb.at[dx * 4 + dy],
                        place.device(dx=dx, dy=dy),
                    )
                )
    total = sb[xh, y * 2 + xl].astype(F32)
    for i, copy in enumerate(arrivals):
        copy.wait_recv()
        total = total + rb[i + 1].astype(F32)
    sz[...] = total.astype(BF)
    last = []
    for dz in range(1, 8):
        last.append(
            net.start(sz.at[lax.rem(z + dz, 8)], zb.at[dz], place.device(dz=dz))
        )
    value = sz[z].astype(F32)
    for dz, copy in enumerate(last):
        copy.wait_recv()
        value = value + zb[dz + 1].astype(F32)
    value = value * (1.0 / (4.0 * NPTS * math.sqrt(NB)))
    out[0, 0] = value[:8]
    out[1, 0] = value[8:]
    net.finish()


def reduce_kernel(e, out, sib, sb, rb, sz, zb, send, recv):
    place = Place()
    net = Copies(send, recv)
    barrier = pltpu.get_barrier_semaphore()
    peers = [place.device(other=True)]
    peers += [place.device(dx=i, dy=j) for i in range(4) for j in range(4) if i or j]
    peers += [place.device(dz=i) for i in range(1, 8)]
    greet(barrier, peers)
    pl.semaphore_wait(barrier, len(peers))
    reduce(place, net, e, sib, sb, rb, sz, zb, out)


VM = pl.BlockSpec(memory_space=pltpu.VMEM)
SM = pl.BlockSpec(memory_space=pltpu.SMEM)
COPIES = 160


def body(wedge_orbitals, star_members, star_ops, rotations, screen_left, screen_right):
    words = jnp.arange(NK, dtype=jnp.int32)[:, None] * 64 + star_ops
    k = jnp.arange(NK, dtype=jnp.int32)[:, None, None]
    code = jnp.sum(jnp.where(star_members[None] == k, words[None], 0), axis=(1, 2))
    sem = pltpu.SemaphoreType.DMA((COPIES,))
    pw, qw, lp = pl.pallas_call(
        gather_kernel,
        out_shape=(
            jax.ShapeDtypeStruct((8, 2, 2, 256, 128), BF),
            jax.ShapeDtypeStruct((2, 18, 4, 4, 16, 128), BF),
            jax.ShapeDtypeStruct((3, 256, 128), BF),
        ),
        in_specs=[VM] * 3,
        out_specs=(VM,) * 3,
        scratch_shapes=[pltpu.VMEM((2, 3, 16, 128), BF), sem, sem],
        compiler_params=pltpu.CompilerParams(
            collective_id=0, has_side_effects=True, vmem_limit_bytes=32 << 20
        ),
    )(wedge_orbitals, screen_left, screen_right)
    e = pl.pallas_call(
        tile_kernel,
        out_shape=jax.ShapeDtypeStruct((NK, 8, 2, 8, 256), F32),
        in_specs=[SM] + [VM] * 4,
        out_specs=VM,
        scratch_shapes=[
            pltpu.VMEM((4, 256, 256), BF),
            pltpu.VMEM((NK, 256, 256), BF),
            pltpu.VMEM((NK, 256, 256), BF),
            pltpu.VMEM((STOPS, 256, 256), F32),
            pltpu.VMEM((NK, 512, 256), F32),
            pltpu.VMEM((2, NK, 256, 256), BF),
        ],
        compiler_params=pltpu.CompilerParams(vmem_limit_bytes=48 << 20),
    )(code, pw, qw, lp, rotations)
    return pl.pallas_call(
        reduce_kernel,
        out_shape=jax.ShapeDtypeStruct((2, 1, 8, 128), F32),
        in_specs=[VM],
        out_specs=VM,
        scratch_shapes=[
            pltpu.VMEM((NK, 8, 8, 256), F32),
            pltpu.VMEM((2, 8, 8, 16, 128), BF),
            pltpu.VMEM((16, 8, 16, 128), BF),
            pltpu.VMEM((8, 16, 128), BF),
            pltpu.VMEM((8, 16, 128), BF),
            sem,
            sem,
        ],
        compiler_params=pltpu.CompilerParams(
            collective_id=1, has_side_effects=True, vmem_limit_bytes=32 << 20
        ),
    )(e)


def solution(mesh):
    return jax.shard_map(
        body,
        mesh=mesh,
        in_specs=(
            P(None, "ka", "pt", None),
            P(),
            P(),
            P(),
            P(None, "pt", None),
            P(None, "pt", None),
        ),
        out_specs=P(None, "ka", "pt", None),
        check_vma=False,
    )
```

```python
import math

import jax
import jax.numpy as jnp
from jax import lax
from jax.experimental import pallas as pl
from jax.experimental.pallas import tpu as pltpu
from jax.sharding import PartitionSpec as P

NB = 128
NPTS = 4096
STOPS = 6
NK = 16
BF = jnp.bfloat16
F32 = jnp.float32
MESH = pl.DeviceIdType.MESH
RING = (0, 1, 7, 2, 6, 3, 5, 4)
GROUPS = ((0, 8, (0, 1, 7)), (8, 12, (2, 6)), (12, 18, (3, 5, 4)))


class Place:
    def __init__(self):
        ka = lax.axis_index("ka")
        pt = lax.axis_index("pt")
        self.xh = lax.div(ka, 8)
        self.z = lax.rem(ka, 8)
        self.y = lax.div(pt, 4)
        self.xl = lax.rem(lax.div(pt, 2), 2)
        self.c = lax.rem(pt, 2)
        self.x = 2 * self.xh + self.xl

    def device(self, dx=0, dy=0, dz=0, other=False):
        x = lax.rem(self.x + dx, 4)
        y = lax.rem(self.y + dy, 4)
        z = lax.rem(self.z + dz, 8)
        c = 1 - self.c if other else self.c
        return (lax.div(x, 2) * 8 + z, y * 4 + lax.rem(x, 2) * 2 + c)

    def swap(self):
        return (self.c * 8 + self.z, self.y * 4 + self.xl * 2 + self.xh)


class Copies:
    def __init__(self, send, recv):
        self.send, self.recv, self.count, self.open = send, recv, 0, []

    def make(self, src, dst, device):
        i = self.count
        self.count += 1
        return pltpu.make_async_remote_copy(
            src_ref=src,
            dst_ref=dst,
            send_sem=self.send.at[i],
            recv_sem=self.recv.at[i],
            device_id=device,
            device_id_type=MESH,
        )

    def start(self, src, dst, device):
        copy = self.make(src, dst, device)
        copy.start()
        self.open.append(copy)
        return copy

    def finish(self):
        for copy in self.open:
            copy.wait_send()


def greet(barrier, devices):
    for device in devices:
        pl.semaphore_signal(barrier, inc=1, device_id=device, device_id_type=MESH)


def stripes(place, net, qw, pw, low, high, rels, row):
    size = high - low
    half = size // 2
    slot = high - 2 * len(rels)
    for rel in rels:
        for u in range(2):
            for ri in range(2):
                qw[ri, slot, 0, 0] = pw[rel, u, ri, pl.ds(row, 16), :]
            slot += 1
    plus = (place.device(dx=1), place.device(dy=1))
    minus = (place.device(dx=3), place.device(dy=3))

    def at(h, first, second, start=low, length=size):
        tiles = pl.ds(start, length)
        if h == 0:
            return qw.at[0, tiles, second, first]
        return qw.at[1, tiles, first, second]

    def second_hop(h, arrived, firsts):
        to, fro = arrived
        to.wait_recv()
        a = net.start(at(h, firsts, 2, low, half), at(h, firsts, 3, low, half), plus[1 - h])
        fro.wait_recv()
        b = net.start(
            at(h, firsts, 1, low + half, half), at(h, firsts, 3, low + half, half), minus[1 - h]
        )
        return a, b

    def across(h, firsts):
        return (
            net.start(at(h, firsts, 0), at(h, firsts, 2), plus[1 - h]),
            net.start(at(h, firsts, 0), at(h, firsts, 1), minus[1 - h]),
        )

    one, two, own = {}, {}, {}
    for h in range(2):
        one[h] = (
            net.start(at(h, 0, 0), at(h, 2, 0), plus[h]),
            net.start(at(h, 0, 0), at(h, 1, 0), minus[h]),
        )
        own[h] = across(h, pl.ds(0, 1))
    yield
    side, last = {}, []
    for h in range(2):
        to, fro = one[h]
        to.wait_recv()
        a = net.start(at(h, 2, 0, low, half), at(h, 3, 0, low, half), plus[h])
        fro.wait_recv()
        b = net.start(
            at(h, 1, 0, low + half, half), at(h, 3, 0, low + half, half), minus[h]
        )
        two[h] = (a, b)
        side[h] = across(h, pl.ds(1, 2))
    for h in range(2):
        last.extend(second_hop(h, own[h], pl.ds(0, 1)))
    yield
    far = {}
    for h in range(2):
        for copy in two[h]:
            copy.wait_recv()
        far[h] = across(h, pl.ds(3, 1))
    for h in range(2):
        last.extend(second_hop(h, side[h], pl.ds(1, 2)))
    yield
    for h in range(2):
        last.extend(second_hop(h, far[h], pl.ds(3, 1)))
    yield
    for copy in last:
        copy.wait_recv()


def prepare(tables, ops, left, right, lp, rt, code, wide, rotations):
    for i in range(3):
        rt[i] = jnp.concatenate([right[2 * i], right[2 * i + 1]], axis=0).T
        lp[1, i] = jnp.concatenate([left[2 * i], left[2 * i + 1]], axis=0).T

    def look(w, words):
        for slot in range(4):
            member = tables[slot, w]
            word = w * 64 + ops[slot, w]
            words = tuple(jnp.where(member == k, word, words[k]) for k in range(NK))
        return words

    words = lax.fori_loop(0, NK, look, (jnp.int32(0),) * NK)
    for k in range(NK):
        code[k] = words[k]


def widen(code, rotations, wide):
    for k in range(NK):
        rotation = rotations[lax.rem(code[k], 64)]
        zero = jnp.zeros_like(rotation)
        wide[k] = jnp.concatenate(
            [jnp.concatenate([rotation, zero], axis=1), jnp.concatenate([zero, rotation], axis=1)],
            axis=0,
        )


def gather(place, net, raw, pw, qw, lp, rt, rown, meanwhile):
    c, xh, z = place.c, place.xh, place.z
    straight = c == xh
    other = place.device(other=True)
    plus, minus = place.device(dz=1), place.device(dz=7)

    swap = net.make(raw, pw.at[0, xh], place.swap())

    @pl.when(c != xh)
    def _():
        swap.start()

    row = pl.multiple_of(32 * z + 16 * c, 16)
    other_row = pl.multiple_of(32 * z + 16 * (1 - c), 16)
    give_left = net.make(lp.at[1], lp.at[0], other)
    give_right = net.make(rown.at[1], rown.at[0], other)

    @pl.when(straight)
    def _():
        for i in range(3):
            rown[0, i] = rt[i, pl.ds(row, 16), :]
            rown[1, i] = rt[i, pl.ds(other_row, 16), :]
        give_right.start()
        give_left.start()
        lp[0] = lp[1]

    @pl.when(c != xh)
    def _():
        swap.wait_recv()

    ups, downs, beside = {}, {}, {}

    def forward(step, ri):
        up, down = (8 - step) % 8, step
        if step < 3 or (step == 3 and ri == 0):
            ups[step, ri] = net.start(pw.at[up, c, ri], pw.at[up - 1 if up else 7, c, ri], plus)
        if step < 3 or (step == 3 and ri == 1):
            downs[step, ri] = net.start(pw.at[down, c, ri], pw.at[down + 1, c, ri], minus)

    def share(rel, ri):
        beside[rel, ri] = net.start(pw.at[rel, c, ri], pw.at[rel, c, ri], other)

    def ring(step):
        for ri in range(2):
            if step < 4:
                ups[step - 1, ri].wait_recv()
                downs[step - 1, ri].wait_recv()
                forward(step, ri)
                share(8 - step, ri)
                share(step, ri)
            else:
                (ups if ri == 0 else downs)[3, ri].wait_recv()
                share(4, ri)

    def shared(rels):
        for rel in rels:
            for ri in range(2):
                beside[rel, ri].wait_recv()

    for ri in range(2):
        forward(0, ri)
        share(0, ri)
    meanwhile()
    ring(1)

    @pl.when(c != xh)
    def _():
        give_right.wait_recv()

    for h, slot, i in ((0, 0, 0), (0, 1, 1), (1, 0, 2), (1, 1, 2)):
        qw[h, slot, 0, 0] = rown[0, i]
    flows = [stripes(place, net, qw, pw, low, high, rels, row) for low, high, rels in GROUPS]

    def advance(g):
        if g >= 0:
            next(flows[g], None)

    shared(GROUPS[0][2])
    advance(0)
    ring(2)
    advance(0)
    shared(GROUPS[1][2])
    advance(1)
    ring(3)
    advance(0)
    advance(1)
    ring(4)
    advance(0)
    shared(GROUPS[2][2])
    advance(2)
    advance(1)
    advance(0)
    advance(2)
    advance(1)
    advance(2)
    advance(1)
    advance(2)
    advance(2)

    @pl.when(c != xh)
    def _():
        give_left.wait_recv()
        swap.wait_send()

    @pl.when(straight)
    def _():
        give_right.wait_send()
        give_left.wait_send()


def dot(a, b, ca, cb):
    return lax.dot_general(a, b, (((ca,), (cb,)), ((), ())), preferred_element_type=F32)


def form_screen(qw, lp, screen):
    lane = lax.broadcasted_iota(jnp.int32, (256, 128), 1)
    for i, (h, slot) in enumerate(((0, 0), (0, 1), (1, 0))):
        factor = qw[h, slot].reshape(256, 128)
        rows = lp[0, i]
        zero = jnp.zeros_like(rows)
        screen[2 * i] = dot(jnp.where(lane < 64, rows, zero), factor, 1, 1)
        screen[2 * i + 1] = dot(jnp.where(lane < 64, zero, rows), factor, 1, 1)


def form_orbitals(z, code, pw, qw, wide, xp, xq):
    for k in range(NK):
        w = lax.div(code[k], 64)
        u = lax.div(w, 8)
        rel = lax.rem(lax.rem(w, 8) - z + 8, 8)
        order = jnp.where(rel == 0, 0, jnp.where(rel <= 4, 2 * rel - 1, 16 - 2 * rel))
        slot = 2 + 2 * order + u
        raw = jnp.concatenate(
            [
                jnp.concatenate([pw[rel, u, 0], pw[rel, u, 1]], axis=1),
                jnp.concatenate(
                    [qw[0, slot].reshape(256, 128), qw[1, slot].reshape(256, 128)], axis=1
                ),
            ],
            axis=0,
        )
        turned = dot(raw, wide[k], 1, 0).astype(BF)
        xp[k] = turned[:256]
        xq[k] = turned[256:]


def form_density(xp, xq, density):
    for k in range(NK):
        rows = xp[k]
        stacked = jnp.concatenate(
            [rows, jnp.concatenate([rows[:, 128:], -rows[:, :128]], axis=1)], axis=0
        )
        density[k] = dot(stacked, xq[k], 1, 1)


def mix(screen, density, mixed):
    def step(t, carry):
        top = pl.multiple_of(t * 16, 16)
        for lanes in (0, 128):
            cols = pl.ds(lanes, 128)
            s = [screen[i, pl.ds(top, 16), cols] for i in range(STOPS)]
            for part in range(2):
                source = pl.multiple_of(part * 256 + top, 16)
                d = [density[j, pl.ds(source, 16), cols] for j in range(NK)]
                for k in range(NK):
                    total = d[(k + 3) % NK] * s[0]
                    for i in range(1, STOPS):
                        total = total + d[(k + 3 - i) % NK] * s[i]
                    mixed[k, pl.ds(top, 16), pl.ds(part * 256 + lanes, 128)] = total.astype(BF)
        return carry

    lax.fori_loop(0, 16, step, 0)


def close(ks, xp, xq, mixed, e):
    for k in ks:
        q = xq[k]
        operand = jnp.concatenate(
            [q, jnp.concatenate([-q[:, 128:], q[:, :128]], axis=1)], axis=0
        )
        y = dot(mixed[k], operand, 1, 0).astype(BF)
        rows = xp[k]
        stacked = jnp.concatenate([rows[:, :128], rows[:, 128:]], axis=0)
        turned = jnp.concatenate([y, jnp.concatenate([y[:, 128:], -y[:, :128]], axis=1)], axis=0)
        e[k] = dot(stacked, turned, 0, 0).reshape(8, 2, 8, 256)


def close_and_reduce(place, net, xp, xq, mixed, e, sib, sb, rb, sz, zb, out):
    c, x, y, z, xh, xl = place.c, place.x, place.y, place.z, place.xh, place.xl
    other = place.device(other=True)

    def hand(half):
        ks = pl.ds(half * 8, 8)
        return net.start(e.at[ks, :, 1 - c], sib.at[ks], other)

    def fold(half, copy):
        copy.wait_recv()
        for i in range(8):
            k = half * 8 + i
            value = e[k, :, c] + sib[k]
            value = jnp.concatenate([value[:, :, :128], value[:, :, 128:]], axis=1)
            sb[half, :, i] = value.astype(BF)

    close(range(8), xp, xq, mixed, e)
    copy = hand(0)
    close(range(8, 12), xp, xq, mixed, e)
    fold(0, copy)
    close(range(12, 16), xp, xq, mixed, e)
    copy = hand(1)
    fold(1, copy)
    arrivals = []
    for dx, dy in PLANE:
        tx = lax.rem(x + dx, 4)
        ty = lax.rem(y + dy, 4)
        arrivals.append(
            net.start(
                sb.at[lax.div(tx, 2), ty * 2 + lax.rem(tx, 2)],
                rb.at[dx * 4 + dy],
                place.device(dx=dx, dy=dy),
            )
        )
    total = sb[xh, y * 2 + xl].astype(F32)
    for (dx, dy), copy in zip(PLANE, arrivals):
        copy.wait_recv()
        total = total + rb[dx * 4 + dy].astype(F32)
    sz[...] = total.astype(BF)
    last = []
    for dz in ZS:
        last.append(net.start(sz.at[lax.rem(z + dz, 8)], zb.at[dz], place.device(dz=dz)))
    value = sz[z].astype(F32)
    for dz, copy in zip(ZS, last):
        copy.wait_recv()
        value = value + zb[dz].astype(F32)
    value = value * (1.0 / (4.0 * NPTS * math.sqrt(NB)))
    out[0, 0] = value[:8]
    out[1, 0] = value[8:]


PLANE = tuple((i, j) for i in range(4) for j in range(4) if i or j)
ZS = (4, 3, 5, 2, 6, 1, 7)


def kernel(
    tables, ops, wedge, rotations, left, right, out,
    raw, pw, qw, lp, rt, rown, code, turns, wide, xp, xq, screen, density, mixed,
    e, sib, sb, rb, sz, zb, send, recv, local,
):
    place = Place()
    net = Copies(send, recv)
    fetch = pltpu.make_async_copy(rotations, turns, local.at[0])
    own = pltpu.make_async_copy(wedge.at[:, 0], raw, local.at[1])
    own.start()
    fetch.start()
    barrier = pltpu.get_barrier_semaphore()
    peers = [place.device(other=True)]
    peers += [place.device(dx=i, dy=j) for i, j in PLANE]
    peers += [place.device(dz=i) for i in ZS]
    greet(barrier, peers)

    @pl.when(place.c != place.xh)
    def _():
        greet(barrier, [place.swap()])

    prepare(tables, ops, left, right, lp, rt, code, wide, rotations)
    own.wait()

    @pl.when(place.c == place.xh)
    def _():
        pw[0, place.c] = raw[...]

    @pl.when(place.c != place.xh)
    def _():
        pl.semaphore_wait(barrier, len(peers) + 1)

    @pl.when(place.c == place.xh)
    def _():
        pl.semaphore_wait(barrier, len(peers))

    def meanwhile():
        fetch.wait()
        widen(code, turns, wide)

    gather(place, net, raw, pw, qw, lp, rt, rown, meanwhile)
    form_screen(qw, lp, screen)
    form_orbitals(place.z, code, pw, qw, wide, xp, xq)
    form_density(xp, xq, density)
    mix(screen, density, mixed)
    close_and_reduce(place, net, xp, xq, mixed, e, sib, sb, rb, sz, zb, out)
    net.finish()


VM = pl.BlockSpec(memory_space=pltpu.VMEM)
SM = pl.BlockSpec(memory_space=pltpu.SMEM)
HB = pl.BlockSpec(memory_space=pl.ANY)
COPIES = 180


def body(wedge_orbitals, star_members, star_ops, rotations, screen_left, screen_right):
    sem = pltpu.SemaphoreType.DMA((COPIES,))
    return pl.pallas_call(
        kernel,
        out_shape=jax.ShapeDtypeStruct((2, 1, 8, 128), F32),
        in_specs=[SM, SM, HB, HB, VM, VM],
        out_specs=VM,
        scratch_shapes=[
            pltpu.VMEM((2, 256, NB), BF),
            pltpu.VMEM((8, 2, 2, 256, 128), BF),
            pltpu.VMEM((2, 18, 4, 4, 16, 128), BF),
            pltpu.VMEM((2, 3, 256, 128), BF),
            pltpu.VMEM((3, 256, 128), BF),
            pltpu.VMEM((2, 3, 16, 128), BF),
            pltpu.SMEM((NK,), jnp.int32),
            pltpu.VMEM((48, NB, NB), BF),
            pltpu.VMEM((NK, 256, 256), BF),
            pltpu.VMEM((NK, 256, 256), BF),
            pltpu.VMEM((NK, 256, 256), BF),
            pltpu.VMEM((STOPS, 256, 256), F32),
            pltpu.VMEM((NK, 512, 256), F32),
            pltpu.VMEM((NK, 256, 512), BF),
            pltpu.VMEM((NK, 8, 2, 8, 256), F32),
            pltpu.VMEM((NK, 8, 8, 256), F32),
            pltpu.VMEM((2, 8, 8, 16, 128), BF),
            pltpu.VMEM((16, 8, 16, 128), BF),
            pltpu.VMEM((8, 16, 128), BF),
            pltpu.VMEM((8, 16, 128), BF),
            sem,
            sem,
            pltpu.SemaphoreType.DMA((2,)),
        ],
        compiler_params=pltpu.CompilerParams(
            collective_id=0, has_side_effects=True, vmem_limit_bytes=56 << 20
        ),
    )(
        star_members.T,
        star_ops.T,
        wedge_orbitals,
        rotations,
        jnp.swapaxes(screen_left, 1, 2),
        jnp.swapaxes(screen_right, 1, 2),
    )


def solution(mesh):
    return jax.shard_map(
        body,
        mesh=mesh,
        in_specs=(
            P(None, "ka", "pt", None),
            P(),
            P(),
            P(),
            P(None, "pt", None),
            P(None, "pt", None),
        ),
        out_specs=P(None, "ka", "pt", None),
        check_vma=False,
    )
```

```python
import math

import jax
import jax.numpy as jnp
from jax import lax
from jax.experimental import pallas as pl
from jax.experimental.pallas import tpu as pltpu
from jax.sharding import PartitionSpec as P

NB = 128
NPTS = 4096
STOPS = 6
NK = 16
BF = jnp.bfloat16
F32 = jnp.float32
MESH = pl.DeviceIdType.MESH
ORDER = (0, 1, 3, 5, 7, 6, 4, 2)
PLANE = tuple((i, j) for i in range(4) for j in range(4) if i or j)
ZS = (4, 3, 5, 2, 6, 1, 7)


class Place:
    def __init__(self):
        ka = lax.axis_index("ka")
        pt = lax.axis_index("pt")
        self.xh = lax.div(ka, 8)
        self.z = lax.rem(ka, 8)
        self.y = lax.div(pt, 4)
        self.xl = lax.rem(lax.div(pt, 2), 2)
        self.c = lax.rem(pt, 2)
        self.x = 2 * self.xh + self.xl

    def device(self, dx=0, dy=0, dz=0, other=False):
        x = lax.rem(self.x + dx, 4)
        y = lax.rem(self.y + dy, 4)
        z = lax.rem(self.z + dz, 8)
        c = 1 - self.c if other else self.c
        return (lax.div(x, 2) * 8 + z, y * 4 + lax.rem(x, 2) * 2 + c)

    def swap(self):
        return (self.c * 8 + self.z, self.y * 4 + self.xl * 2 + self.xh)

    def taker(self, dz, flip):
        core = 1 - self.c if flip else self.c
        return (self.c * 8 + lax.rem(self.z + dz, 8), self.y * 4 + self.xl * 2 + core)

    def giver(self, u, dz):
        return (u * 8 + lax.rem(self.z + dz, 8), self.y * 4 + self.xl * 2 + self.xh)


class Copies:
    def __init__(self, send, recv):
        self.send, self.recv, self.count, self.open = send, recv, 0, []

    def make(self, src, dst, device):
        i = self.count
        self.count += 1
        return pltpu.make_async_remote_copy(
            src_ref=src,
            dst_ref=dst,
            send_sem=self.send.at[i],
            recv_sem=self.recv.at[i],
            device_id=device,
            device_id_type=MESH,
        )

    def start(self, src, dst, device):
        copy = self.make(src, dst, device)
        copy.start()
        self.open.append(copy)
        return copy

    def finish(self):
        for copy in self.open:
            copy.wait_send()


def greet(barrier, devices):
    for device in devices:
        pl.semaphore_signal(barrier, inc=1, device_id=device, device_id_type=MESH)


def factors(left, right, lp, rt):
    for i in range(3):
        rt[i] = jnp.concatenate([right[2 * i], right[2 * i + 1]], axis=0).T
    for i in range(3):
        lp[1, i] = jnp.concatenate([left[2 * i], left[2 * i + 1]], axis=0).T


def decode(tables, ops, code):
    def look(w, words):
        for slot in range(4):
            member = tables[slot, w]
            word = w * 64 + ops[slot, w]
            words = tuple(jnp.where(member == k, word, words[k]) for k in range(NK))
        return words

    words = lax.fori_loop(0, NK, look, (jnp.int32(0),) * NK)
    for k in range(NK):
        code[k] = words[k]


def widen(code, rotations, wide):
    for k in range(NK):
        rotation = rotations[lax.rem(code[k], 64)]
        zero = jnp.zeros_like(rotation)
        wide[k] = jnp.concatenate(
            [jnp.concatenate([rotation, zero], axis=1), jnp.concatenate([zero, rotation], axis=1)],
            axis=0,
        )


def gather(
    place, net, raw, pw, qw, lp, rt, rown, stripe_send, stripe_recv, prepare, meanwhile
):
    c, xh, z = place.c, place.xh, place.z
    straight = c == xh
    other = place.device(other=True)
    plus, minus = place.device(dz=1), place.device(dz=7)

    def stripe(dz, flip):
        target = lax.rem(z + dz, 8)
        core = 1 - c if flip else c
        row = pl.multiple_of(32 * target + 16 * core, 16)
        slot = 2 + 2 * ORDER[(8 - dz) % 8] + xh
        return pltpu.make_async_remote_copy(
            src_ref=raw.at[:, pl.ds(row, 16), :],
            dst_ref=qw.at[:, slot, 0, 0],
            send_sem=stripe_send.at[dz, flip],
            recv_sem=stripe_recv.at[dz, xh],
            device_id=place.taker(dz, flip),
            device_id_type=MESH,
        )

    def stripe_arrival(dz, u):
        return pltpu.make_async_remote_copy(
            src_ref=raw.at[:, pl.ds(0, 16), :],
            dst_ref=qw.at[:, 2 + 2 * ORDER[(8 - dz) % 8] + u, 0, 0],
            send_sem=stripe_send.at[dz, u],
            recv_sem=stripe_recv.at[dz, u],
            device_id=other,
            device_id_type=MESH,
        )

    for dz in ZS:
        for flip in range(2):
            stripe(dz, flip).start()
    stripe(0, 1).start()
    swap = net.make(raw, pw.at[0, xh], place.swap())
    own_row = pl.multiple_of(32 * z + 16 * c, 16)
    other_row = pl.multiple_of(32 * z + 16 * (1 - c), 16)

    @pl.when(c != xh)
    def _():
        stripe(0, 0).start()
        swap.start()

    ups, downs, beside = {}, {}, {}

    def forward(step, ri):
        up, down = (8 - step) % 8, step
        if step < 3 or (step == 3 and ri == 0):
            ups[step, ri] = net.make(pw.at[up, c, ri], pw.at[up - 1 if up else 7, c, ri], plus)
        if step < 3 or (step == 3 and ri == 1):
            downs[step, ri] = net.make(pw.at[down, c, ri], pw.at[down + 1, c, ri], minus)
        return [group[step, ri] for group in (ups, downs) if (step, ri) in group]

    def share(rel, ri):
        beside[rel, ri] = net.make(pw.at[rel, c, ri], pw.at[rel, c, ri], other)
        return [beside[rel, ri]]

    def launch(copies, keep=True):
        for copy in copies:
            copy.start()
        if keep:
            net.open.extend(copies)

    first = []
    for ri in range(2):
        first += forward(0, ri)
    for ri in range(2):
        first += share(0, ri)
    net.open.extend(first)

    @pl.when(straight)
    def _():
        pw[0, c] = raw[...]
        qw[:, 2 + c, 0, 0] = raw[:, pl.ds(own_row, 16), :]
        launch(first, False)

    prepare()
    give_left = net.make(lp.at[1], lp.at[0], other)
    give_right = net.make(rown.at[1], rown.at[0], other)

    @pl.when(straight)
    def _():
        for i in range(3):
            rown[0, i] = rt[i, pl.ds(own_row, 16), :]
            rown[1, i] = rt[i, pl.ds(other_row, 16), :]
        give_right.start()
        give_left.start()
        lp[0] = lp[1]

    @pl.when(c != xh)
    def _():
        swap.wait_recv()
        launch(first, False)
        give_right.wait_recv()

    for h, slot, i in ((0, 0, 0), (0, 1, 1), (1, 0, 2), (1, 1, 2)):
        qw[h, slot, 0, 0] = rown[0, i]
    for dz in (0, 1, 7, 2, 6, 3, 5, 4):
        for u in range(2):
            if dz:
                stripe_arrival(dz, u).wait_recv()
            else:

                @pl.when(jnp.logical_or(c != xh, u != xh))
                def _():
                    stripe_arrival(dz, u).wait_recv()

    def own(h, to, **step):
        return net.start(qw.at[h, :, 0, 0], qw.at[h, :, to[0], to[1]], place.device(**step))

    rows, columns, rest, last = {}, {}, [], []
    for d in (2, 1, 3):
        rows[d] = own(0, (0, 4 - d), dx=d)
        columns[d] = own(1, (4 - d, 0), dy=d)
    for d in (2, 1, 3):
        rest.append(own(1, (0, 4 - d), dx=d))
        rest.append(own(0, (4 - d, 0), dy=d))

    def ring(step):
        for ri in range(2):
            if step < 4:
                ups[step - 1, ri].wait_recv()
                downs[step - 1, ri].wait_recv()
                launch(forward(step, ri) + share(8 - step, ri) + share(step, ri))
            else:
                (ups if ri == 0 else downs)[3, ri].wait_recv()
                launch(share(4, ri))

    ring(1)
    meanwhile()
    for d in (1, 3, 2):
        rows[d].wait_recv()
        for dy in (2, 1, 3):
            last.append(
                net.start(
                    qw.at[0, :, 0, 4 - d], qw.at[0, :, 4 - dy, 4 - d], place.device(dy=dy)
                )
            )
        columns[d].wait_recv()
        for dx in (2, 1, 3):
            last.append(
                net.start(
                    qw.at[1, :, 4 - d, 0], qw.at[1, :, 4 - d, 4 - dx], place.device(dx=dx)
                )
            )
    ring(2)
    ring(3)
    ring(4)
    for copy in rest + last + list(beside.values()):
        copy.wait_recv()

    @pl.when(c != xh)
    def _():
        give_left.wait_recv()
        swap.wait_send()
        stripe(0, 0).wait_send()

    @pl.when(straight)
    def _():
        give_right.wait_send()
        give_left.wait_send()

    for dz in ZS:
        for flip in range(2):
            stripe(dz, flip).wait_send()
    stripe(0, 1).wait_send()


def dot(a, b, ca, cb):
    return lax.dot_general(a, b, (((ca,), (cb,)), ((), ())), preferred_element_type=F32)


def form_screen(qw, lp, screen):
    lane = lax.broadcasted_iota(jnp.int32, (256, 128), 1)
    for i, (h, slot) in enumerate(((0, 0), (0, 1), (1, 0))):
        factor = qw[h, slot].reshape(256, 128)
        rows = lp[0, i]
        zero = jnp.zeros_like(rows)
        screen[2 * i] = dot(jnp.where(lane < 64, rows, zero), factor, 1, 1)
        screen[2 * i + 1] = dot(jnp.where(lane < 64, zero, rows), factor, 1, 1)


def form_orbitals(z, code, pw, qw, wide, xp, xq):
    for k in range(NK):
        w = lax.div(code[k], 64)
        u = lax.div(w, 8)
        rel = lax.rem(lax.rem(w, 8) - z + 8, 8)
        order = jnp.where(rel == 0, 0, jnp.where(rel <= 4, 2 * rel - 1, 16 - 2 * rel))
        slot = 2 + 2 * order + u
        raw = jnp.concatenate(
            [
                jnp.concatenate([pw[rel, u, 0], pw[rel, u, 1]], axis=1),
                jnp.concatenate(
                    [qw[0, slot].reshape(256, 128), qw[1, slot].reshape(256, 128)], axis=1
                ),
            ],
            axis=0,
        )
        turned = dot(raw, wide[k], 1, 0).astype(BF)
        xp[k] = turned[:256]
        xq[k] = turned[256:]


def form_density(xp, xq, density):
    for k in range(NK):
        rows = xp[k]
        stacked = jnp.concatenate(
            [rows, jnp.concatenate([rows[:, 128:], -rows[:, :128]], axis=1)], axis=0
        )
        density[k] = dot(stacked, xq[k], 1, 1)


def mix(screen, density, mixed, xp, xpt):
    def step(t, carry):
        rows = xp[t]
        xpt[t] = jnp.concatenate([rows[:, :128], rows[:, 128:]], axis=0).T
        top = pl.multiple_of(t * 16, 16)
        for lanes in (0, 128):
            cols = pl.ds(lanes, 128)
            s = [screen[i, pl.ds(top, 16), cols] for i in range(STOPS)]
            for part in range(2):
                source = pl.multiple_of(part * 256 + top, 16)
                d = [density[j, pl.ds(source, 16), cols] for j in range(NK)]
                for k in range(NK):
                    total = d[(k + 3) % NK] * s[0]
                    for i in range(1, STOPS):
                        total = total + d[(k + 3 - i) % NK] * s[i]
                    mixed[k, pl.ds(top, 16), pl.ds(part * 256 + lanes, 128)] = total.astype(BF)
        return carry

    lax.fori_loop(0, 16, step, 0)


def close(ks, xpt, xq, mixed, e):
    for k in ks:
        q = xq[k]
        operand = jnp.concatenate(
            [q, jnp.concatenate([-q[:, 128:], q[:, :128]], axis=1)], axis=0
        )
        y = dot(mixed[k], operand, 1, 0).astype(BF)
        turned = jnp.concatenate([y, jnp.concatenate([y[:, 128:], -y[:, :128]], axis=1)], axis=0)
        e[k] = dot(xpt[k], turned, 1, 0).reshape(8, 2, 8, 256)


def close_and_reduce(place, net, xpt, xq, mixed, e, sib, sb, rb, sz, zb, out):
    c, x, y, z, xh, xl = place.c, place.x, place.y, place.z, place.xh, place.xl
    other = place.device(other=True)

    def batch(b):
        return [8 * h + b * SIZE + i for h in range(2) for i in range(SIZE)]

    def hand(b):
        copies = []
        for h in range(2):
            ks = pl.ds(8 * h + b * SIZE, SIZE)
            copies.append(net.start(e.at[ks, :, 1 - c], sib.at[ks], other))
        return copies

    def fold(b, copies):
        for h in range(2):
            copies[h].wait_recv()
            for i in range(b * SIZE, (b + 1) * SIZE):
                value = e[8 * h + i, :, c] + sib[8 * h + i]
                value = jnp.concatenate([value[:, :, :128], value[:, :, 128:]], axis=1)
                sb[h, :, i] = value.astype(BF)

    def scatter(b):
        copies = []
        zz = pl.ds(b * SIZE, SIZE)
        for dx, dy in FAR_FIRST:
            tx = lax.rem(x + dx, 4)
            ty = lax.rem(y + dy, 4)
            copies.append(
                net.start(
                    sb.at[lax.div(tx, 2), ty * 2 + lax.rem(tx, 2), zz],
                    rb.at[dx * 4 + dy, zz],
                    place.device(dx=dx, dy=dy),
                )
            )
        return copies

    def collect(b, copies):
        zz = pl.ds(b * SIZE, SIZE)
        total = sb[xh, y * 2 + xl, zz].astype(F32)
        for (dx, dy), copy in zip(reversed(FAR_FIRST), reversed(copies)):
            copy.wait_recv()
            total = total + rb[dx * 4 + dy, zz].astype(F32)
        sz[zz] = total.astype(BF)

    handed, sent = {}, {}
    for b in range(BATCHES):
        ks = batch(b)
        close(ks[:SIZE], xpt, xq, mixed, e)
        if b:
            fold(b - 1, handed[b - 1])
            sent[b - 1] = scatter(b - 1)
        close(ks[SIZE:], xpt, xq, mixed, e)
        handed[b] = hand(b)
    fold(BATCHES - 1, handed[BATCHES - 1])
    sent[BATCHES - 1] = scatter(BATCHES - 1)
    for b in range(BATCHES):
        collect(b, sent[b])
    last = []
    for dz in ZS:
        last.append(net.start(sz.at[lax.rem(z + dz, 8)], zb.at[dz], place.device(dz=dz)))
    value = sz[z].astype(F32)
    for dz, copy in zip(ZS, last):
        copy.wait_recv()
        value = value + zb[dz].astype(F32)
    value = value * (1.0 / (4.0 * NPTS * math.sqrt(NB)))
    out[0, 0] = value[:8]
    out[1, 0] = value[8:]


FAR_FIRST = tuple(sorted(PLANE, key=lambda d: -min(d[0], 4 - d[0]) - min(d[1], 4 - d[1])))
BATCHES = 2
SIZE = 8 // BATCHES


def kernel(
    star, star_op, wedge, rotations, screen_left, screen_right, out,
    tables, ops, left, right, raw, pw, qw, lp, rt, rown, code, turns, wide, xp, xpt, xq, screen,
    density, mixed, e, sib, sb, rb, sz, zb, send, recv, stripe_send, stripe_recv, local,
):
    place = Place()
    net = Copies(send, recv)
    fetches = [
        pltpu.make_async_copy(source, target, local.at[i])
        for i, (source, target) in enumerate(
            (
                (wedge.at[:, 0], raw),
                (screen_right, right),
                (screen_left, left),
                (star, tables),
                (star_op, ops),
                (rotations, turns),
            )
        )
    ]
    for fetch in fetches:
        fetch.start()
    barrier = pltpu.get_barrier_semaphore()
    peers = [place.device(other=True), place.device(dz=1), place.device(dz=7)]
    peers += [place.device(dx=d) for d in (1, 2, 3)] + [place.device(dy=d) for d in (1, 2, 3)]
    peers += [place.giver(u, dz) for dz in range(1, 8) for u in range(2)]
    greet(barrier, peers)
    greet(barrier, [place.giver(1 - place.xh, 0)])

    @pl.when(place.c != place.xh)
    def _():
        greet(barrier, [place.swap(), place.giver(place.xh, 0)])

    fetches[0].wait()

    @pl.when(place.c != place.xh)
    def _():
        pl.semaphore_wait(barrier, len(peers) + 3)

    @pl.when(place.c == place.xh)
    def _():
        pl.semaphore_wait(barrier, len(peers) + 1)

    def prepare():
        fetches[1].wait()
        fetches[2].wait()
        factors(left, right, lp, rt)

    def meanwhile():
        for fetch in fetches[3:]:
            fetch.wait()
        decode(tables, ops, code)
        widen(code, turns, wide)

    gather(
        place, net, raw, pw, qw, lp, rt, rown, stripe_send, stripe_recv, prepare, meanwhile
    )
    form_screen(qw, lp, screen)
    form_orbitals(place.z, code, pw, qw, wide, xp, xq)
    form_density(xp, xq, density)
    mix(screen, density, mixed, xp, xpt)
    close_and_reduce(place, net, xpt, xq, mixed, e, sib, sb, rb, sz, zb, out)
    net.finish()


VM = pl.BlockSpec(memory_space=pltpu.VMEM)
HB = pl.BlockSpec(memory_space=pl.ANY)
COPIES = 180


def body(wedge_orbitals, star_members, star_ops, rotations, screen_left, screen_right):
    sem = pltpu.SemaphoreType.DMA((COPIES,))
    return pl.pallas_call(
        kernel,
        out_shape=jax.ShapeDtypeStruct((2, 1, 8, 128), F32),
        in_specs=[HB] * 6,
        out_specs=VM,
        scratch_shapes=[
            pltpu.SMEM((4, NK), jnp.int32),
            pltpu.SMEM((4, NK), jnp.int32),
            pltpu.VMEM((STOPS, 64, 256), BF),
            pltpu.VMEM((STOPS, 64, 256), BF),
            pltpu.VMEM((2, 256, NB), BF),
            pltpu.VMEM((8, 2, 2, 256, 128), BF),
            pltpu.VMEM((2, 18, 4, 4, 16, 128), BF),
            pltpu.VMEM((2, 3, 256, 128), BF),
            pltpu.VMEM((3, 256, 128), BF),
            pltpu.VMEM((2, 3, 16, 128), BF),
            pltpu.SMEM((NK,), jnp.int32),
            pltpu.VMEM((48, NB, NB), BF),
            pltpu.VMEM((NK, 256, 256), BF),
            pltpu.VMEM((NK, 256, 256), BF),
            pltpu.VMEM((NK, NB, 512), BF),
            pltpu.VMEM((NK, 256, 256), BF),
            pltpu.VMEM((STOPS, 256, 256), F32),
            pltpu.VMEM((NK, 512, 256), F32),
            pltpu.VMEM((NK, 256, 512), BF),
            pltpu.VMEM((NK, 8, 2, 8, 256), F32),
            pltpu.VMEM((NK, 8, 8, 256), F32),
            pltpu.VMEM((2, 8, 8, 16, 128), BF),
            pltpu.VMEM((16, 8, 16, 128), BF),
            pltpu.VMEM((8, 16, 128), BF),
            pltpu.VMEM((8, 16, 128), BF),
            sem,
            sem,
            pltpu.SemaphoreType.DMA((8, 2)),
            pltpu.SemaphoreType.DMA((8, 2)),
            pltpu.SemaphoreType.DMA((6,)),
        ],
        compiler_params=pltpu.CompilerParams(
            collective_id=0, has_side_effects=True, vmem_limit_bytes=56 << 20
        ),
    )(
        star_members.T,
        star_ops.T,
        wedge_orbitals,
        rotations,
        jnp.swapaxes(screen_left, 1, 2),
        jnp.swapaxes(screen_right, 1, 2),
    )


def solution(mesh):
    return jax.shard_map(
        body,
        mesh=mesh,
        in_specs=(
            P(None, "ka", "pt", None),
            P(),
            P(),
            P(),
            P(None, "pt", None),
            P(None, "pt", None),
        ),
        out_specs=P(None, "ka", "pt", None),
        check_vma=False,
    )
```

```python
import math

import jax
import jax.numpy as jnp
from jax import lax
from jax.experimental import pallas as pl
from jax.experimental.pallas import tpu as pltpu
from jax.sharding import PartitionSpec as P

NB = 128
NPTS = 4096
STOPS = 6
NK = 16
BF = jnp.bfloat16
F32 = jnp.float32
MESH = pl.DeviceIdType.MESH
PLANE = tuple((i, j) for i in range(4) for j in range(4) if i or j)
ZS = (4, 3, 5, 2, 6, 1, 7)


class Place:
    def __init__(self):
        ka = lax.axis_index("ka")
        pt = lax.axis_index("pt")
        self.xh = lax.div(ka, 8)
        self.z = lax.rem(ka, 8)
        self.y = lax.div(pt, 4)
        self.xl = lax.rem(lax.div(pt, 2), 2)
        self.c = lax.rem(pt, 2)
        self.x = 2 * self.xh + self.xl

    def device(self, dx=0, dy=0, dz=0, other=False):
        x = lax.rem(self.x + dx, 4)
        y = lax.rem(self.y + dy, 4)
        z = lax.rem(self.z + dz, 8)
        c = 1 - self.c if other else self.c
        return (lax.div(x, 2) * 8 + z, y * 4 + lax.rem(x, 2) * 2 + c)

    def swap(self):
        return (self.c * 8 + self.z, self.y * 4 + self.xl * 2 + self.xh)


class Copies:
    def __init__(self, send, recv):
        self.send, self.recv, self.count, self.open = send, recv, 0, []

    def make(self, src, dst, device):
        i = self.count
        self.count += 1
        return pltpu.make_async_remote_copy(
            src_ref=src,
            dst_ref=dst,
            send_sem=self.send.at[i],
            recv_sem=self.recv.at[i],
            device_id=device,
            device_id_type=MESH,
        )

    def start(self, src, dst, device):
        copy = self.make(src, dst, device)
        copy.start()
        self.open.append(copy)
        return copy

    def finish(self):
        for copy in self.open:
            copy.wait_send()


def greet(barrier, devices):
    for device in devices:
        pl.semaphore_signal(barrier, inc=1, device_id=device, device_id_type=MESH)


def factors(left, right, lp, rt):
    for i in range(3):
        rt[i] = jnp.concatenate([right[2 * i], right[2 * i + 1]], axis=0).T
    for i in range(3):
        lp[1, i] = jnp.concatenate([left[2 * i], left[2 * i + 1]], axis=0).T


def decode(tables, ops, code):
    def look(w, words):
        for slot in range(4):
            member = tables[slot, w]
            word = w * 64 + ops[slot, w]
            words = tuple(jnp.where(member == k, word, words[k]) for k in range(NK))
        return words

    words = lax.fori_loop(0, NK, look, (jnp.int32(0),) * NK)
    for k in range(NK):
        code[k] = words[k]


def widen(code, rotations, wide):
    for k in range(NK):
        rotation = rotations[lax.rem(code[k], 64)]
        zero = jnp.zeros_like(rotation)
        wide[k] = jnp.concatenate(
            [jnp.concatenate([rotation, zero], axis=1), jnp.concatenate([zero, rotation], axis=1)],
            axis=0,
        )


def gather(
    place, net, raw, pw, qw, rq, lp, rt, rown, stripe_send, stripe_recv, prepare, meanwhile, turn_rows
):
    c, xh, xl, z = place.c, place.xh, place.xl, place.z
    straight = c == xh
    other = place.device(other=True)
    plus, minus = place.device(dz=1), place.device(dz=7)

    def stripe(dz, flip):
        core = 1 - c if flip else c
        row = pl.multiple_of(32 * lax.rem(z + dz, 8) + 16 * core, 16)
        return pltpu.make_async_remote_copy(
            src_ref=raw.at[:, pl.ds(row, 16), :],
            dst_ref=qw.at[:, 0, (8 - dz) % 8, 0, 0, c],
            send_sem=stripe_send.at[dz, flip],
            recv_sem=stripe_recv.at[dz, c],
            device_id=place.device(dz=dz, other=bool(flip)),
            device_id_type=MESH,
        )

    def stripe_arrival(dz, core):
        return pltpu.make_async_remote_copy(
            src_ref=raw.at[:, pl.ds(0, 16), :],
            dst_ref=qw.at[:, 0, (8 - dz) % 8, 0, 0, core],
            send_sem=stripe_send.at[dz, core],
            recv_sem=stripe_recv.at[dz, core],
            device_id=other,
            device_id_type=MESH,
        )

    for dz in ZS:
        for flip in range(2):
            stripe(dz, flip).start()
    stripe(0, 1).start()
    swap = net.make(raw, pw.at[0, xh], place.swap())
    own_row = pl.multiple_of(32 * z + 16 * c, 16)
    other_row = pl.multiple_of(32 * z + 16 * (1 - c), 16)

    @pl.when(c != xh)
    def _():
        swap.start()

    qw[:, 0, 0, 0, 0, c] = raw[:, pl.ds(own_row, 16), :]

    ups, downs, beside = {}, {}, {}

    def forward(step, ri):
        up, down = (8 - step) % 8, step
        if step < 3 or (step == 3 and ri == 0):
            ups[step, ri] = net.make(pw.at[up, c, ri], pw.at[up - 1 if up else 7, c, ri], plus)
        if step < 3 or (step == 3 and ri == 1):
            downs[step, ri] = net.make(pw.at[down, c, ri], pw.at[down + 1, c, ri], minus)
        return [group[step, ri] for group in (ups, downs) if (step, ri) in group]

    def share(rel, ri):
        beside[rel, ri] = net.make(pw.at[rel, c, ri], pw.at[rel, c, ri], other)
        return [beside[rel, ri]]

    def launch(copies, keep=True):
        for copy in copies:
            copy.start()
        if keep:
            net.open.extend(copies)

    first = []
    for ri in range(2):
        first += forward(0, ri)
    for ri in range(2):
        first += share(0, ri)
    net.open.extend(first)

    @pl.when(straight)
    def _():
        pw[0, c] = raw[...]
        launch(first, False)

    prepare()
    give_left = net.make(lp.at[1], lp.at[0], other)
    give_right = net.make(rown.at[1], rown.at[0], other)

    @pl.when(straight)
    def _():
        for i in range(3):
            rown[0, i] = rt[i, pl.ds(own_row, 16), :]
            rown[1, i] = rt[i, pl.ds(other_row, 16), :]
        give_right.start()
        give_left.start()
        lp[0] = lp[1]

    @pl.when(c != xh)
    def _():
        swap.wait_recv()
        launch(first, False)
        give_right.wait_recv()

    rq[:, 0, 0, xh] = rown[0]
    for dz in (0, 1, 7, 2, 6, 3, 5, 4):
        for core in range(2):
            if dz:
                stripe_arrival(dz, core).wait_recv()
    stripe_arrival(0, 1 - c).wait_recv()

    turned_x = (0, xl, 1, 1 - xl)

    def tile(h, px, py):
        return qw.at[h, turned_x[px], :, py, px % 2]

    def sent_tile(h, px, py, dx, dy):
        qx, qy = (px + 4 - dx) % 4, (py + 4 - dy) % 4
        there = lax.rem(xl + dx, 2)
        turned = (0, there, 1, 1 - there)[qx]
        return qw.at[h, turned, :, qy, qx % 2]

    def pass_on(h, px, py, dx, dy):
        return net.start(tile(h, px, py), sent_tile(h, px, py, dx, dy), place.device(dx=dx, dy=dy))

    rows, columns, factor, rest, last = {}, {}, {}, [], []
    for d in (2, 1, 3):
        rows[d] = pass_on(0, 0, 0, d, 0)
        columns[d] = pass_on(1, 0, 0, 0, d)
    for d in (2, 1, 3):
        factor[d] = net.start(rq.at[:, 0, 0, xh], rq.at[:, 4 - d, 0, xh], place.device(dy=d))
    for d in (2, 1, 3):
        rest.append(pass_on(1, 0, 0, d, 0))
        rest.append(pass_on(0, 0, 0, 0, d))

    def ring(step):
        for ri in range(2):
            if step < 4:
                ups[step - 1, ri].wait_recv()
                downs[step - 1, ri].wait_recv()
                launch(forward(step, ri) + share(8 - step, ri) + share(step, ri))
            else:
                (ups if ri == 0 else downs)[3, ri].wait_recv()
                launch(share(4, ri))

    ring(1)
    meanwhile()
    for d in (1, 3, 2):
        rows[d].wait_recv()
        for dy in (2, 1, 3):
            last.append(pass_on(0, 4 - d, 0, 0, dy))
        columns[d].wait_recv()
        for dx in (2, 1, 3):
            last.append(pass_on(1, 0, 4 - d, dx, 0))
        factor[d].wait_recv()
    for dx in (2, 1, 3):
        last.append(
            net.start(
                rq.at[:, :, 0, xh], rq.at[:, :, (4 - dx) % 2, xh], place.device(dx=dx)
            )
        )
    ring(2)
    ring(3)
    ring(4)
    for copy in beside.values():
        copy.wait_recv()
    turn_rows()
    for copy in rest + last:
        copy.wait_recv()

    @pl.when(c != xh)
    def _():
        give_left.wait_recv()
        swap.wait_send()

    @pl.when(straight)
    def _():
        give_right.wait_send()
        give_left.wait_send()

    for dz in ZS:
        for flip in range(2):
            stripe(dz, flip).wait_send()
    stripe(0, 1).wait_send()


def dot(a, b, ca, cb):
    return lax.dot_general(a, b, (((ca,), (cb,)), ((), ())), preferred_element_type=F32)


def form_screen(rq, lp, screen):
    lane = lax.broadcasted_iota(jnp.int32, (256, 128), 1)
    for i in range(3):
        factor = rq[i].reshape(256, 128)
        rows = lp[0, i]
        zero = jnp.zeros_like(rows)
        screen[2 * i] = dot(jnp.where(lane < 64, rows, zero), factor, 1, 1)
        screen[2 * i + 1] = dot(jnp.where(lane < 64, zero, rows), factor, 1, 1)


def seat(z, word):
    w = lax.div(word, 64)
    return lax.div(w, 8), lax.rem(lax.rem(w, 8) - z + 8, 8)


def form_rows(z, code, pw, wide, xp, xpt):
    for k in range(NK):
        u, rel = seat(z, code[k])
        raw = jnp.concatenate([pw[rel, u, 0], pw[rel, u, 1]], axis=1)
        turned = dot(raw, wide[k], 1, 0).astype(BF)
        xp[k] = turned
        xpt[k] = jnp.concatenate([turned[:, :128], turned[:, 128:]], axis=0).T


def form_columns(place, code, qw, wide, xq):
    for k in range(NK):
        u, rel = seat(place.z, code[k])
        turned = jnp.where(u == place.xh, 0, 1)
        raw = jnp.concatenate(
            [
                qw[0, turned, rel].reshape(256, 128),
                qw[1, turned, rel].reshape(256, 128),
            ],
            axis=1,
        )
        xq[k] = dot(raw, wide[k], 1, 0).astype(BF)


def form_density(xp, xq, density):
    for k in range(NK):
        rows = xp[k]
        stacked = jnp.concatenate(
            [rows, jnp.concatenate([rows[:, 128:], -rows[:, :128]], axis=1)], axis=0
        )
        density[k] = dot(stacked, xq[k], 1, 1)


def mix(screen, density, mixed):
    def step(t, carry):
        top = pl.multiple_of(t * 16, 16)
        for lanes in (0, 128):
            cols = pl.ds(lanes, 128)
            s = [screen[i, pl.ds(top, 16), cols] for i in range(STOPS)]
            for part in range(2):
                source = pl.multiple_of(part * 256 + top, 16)
                d = [density[j, pl.ds(source, 16), cols] for j in range(NK)]
                for k in range(NK):
                    total = d[(k + 3) % NK] * s[0]
                    for i in range(1, STOPS):
                        total = total + d[(k + 3 - i) % NK] * s[i]
                    mixed[k, pl.ds(top, 16), pl.ds(part * 256 + lanes, 128)] = total.astype(BF)
        return carry

    lax.fori_loop(0, 16, step, 0)


def close(ks, xpt, xq, mixed, e):
    ys = []
    for k in ks:
        q = xq[k]
        operand = jnp.concatenate(
            [q, jnp.concatenate([-q[:, 128:], q[:, :128]], axis=1)], axis=0
        )
        ys.append(dot(mixed[k], operand, 1, 0).astype(BF))
    for k, y in zip(ks, ys):
        turned = jnp.concatenate([y, jnp.concatenate([y[:, 128:], -y[:, :128]], axis=1)], axis=0)
        e[k] = dot(xpt[k], turned, 1, 0).reshape(8, 2, 8, 256)


def close_and_reduce(place, net, xpt, xq, mixed, e, sib, sb, rb, sz, zb, out):
    c, x, y, z, xh, xl = place.c, place.x, place.y, place.z, place.xh, place.xl
    other = place.device(other=True)

    def batch(b):
        return [8 * h + b * SIZE + i for h in range(2) for i in range(SIZE)]

    def hand(b):
        copies = []
        for h in range(2):
            ks = pl.ds(8 * h + b * SIZE, SIZE)
            copies.append(net.start(e.at[ks, :, 1 - c], sib.at[ks], other))
        return copies

    def fold(b, copies):
        for h in range(2):
            copies[h].wait_recv()
            for i in range(b * SIZE, (b + 1) * SIZE):
                value = e[8 * h + i, :, c] + sib[8 * h + i]
                value = jnp.concatenate([value[:, :, :128], value[:, :, 128:]], axis=1)
                sb[h, :, i] = value.astype(BF)

    def scatter(b):
        copies = []
        zz = pl.ds(b * SIZE, SIZE)
        for dx, dy in FAR_FIRST:
            tx = lax.rem(x + dx, 4)
            ty = lax.rem(y + dy, 4)
            copies.append(
                net.start(
                    sb.at[lax.div(tx, 2), ty * 2 + lax.rem(tx, 2), zz],
                    rb.at[dx * 4 + dy, zz],
                    place.device(dx=dx, dy=dy),
                )
            )
        return copies

    def collect(b, copies):
        zz = pl.ds(b * SIZE, SIZE)
        total = sb[xh, y * 2 + xl, zz].astype(F32)
        for (dx, dy), copy in zip(reversed(FAR_FIRST), reversed(copies)):
            copy.wait_recv()
            total = total + rb[dx * 4 + dy, zz].astype(F32)
        sz[zz] = total.astype(BF)

    handed, sent = {}, {}
    for b in range(BATCHES):
        ks = batch(b)
        close(ks[:SIZE], xpt, xq, mixed, e)
        if b:
            fold(b - 1, handed[b - 1])
            sent[b - 1] = scatter(b - 1)
        close(ks[SIZE:], xpt, xq, mixed, e)
        handed[b] = hand(b)
    fold(BATCHES - 1, handed[BATCHES - 1])
    sent[BATCHES - 1] = scatter(BATCHES - 1)
    for b in range(BATCHES):
        collect(b, sent[b])
    last = []
    for dz in ZS:
        last.append(net.start(sz.at[lax.rem(z + dz, 8)], zb.at[dz], place.device(dz=dz)))
    value = sz[z].astype(F32)
    for dz, copy in zip(ZS, last):
        copy.wait_recv()
        value = value + zb[dz].astype(F32)
    value = value * (1.0 / (4.0 * NPTS * math.sqrt(NB)))
    out[0, 0] = value[:8]
    out[1, 0] = value[8:]


FAR_FIRST = tuple(sorted(PLANE, key=lambda d: -min(d[0], 4 - d[0]) - min(d[1], 4 - d[1])))
BATCHES = 2
SIZE = 8 // BATCHES


def kernel(
    star, star_op, wedge, rotations, screen_left, screen_right, out,
    tables, ops, left, right, raw, pw, qw, rq, lp, rt, rown, code, turns, wide, xp, xpt, xq, screen,
    density, mixed, e, sib, sb, rb, sz, zb, send, recv, stripe_send, stripe_recv, local,
):
    place = Place()
    net = Copies(send, recv)
    fetches = [
        pltpu.make_async_copy(source, target, local.at[i])
        for i, (source, target) in enumerate(
            (
                (wedge.at[:, 0], raw),
                (screen_right, right),
                (screen_left, left),
                (star, tables),
                (star_op, ops),
                (rotations, turns),
            )
        )
    ]
    for fetch in fetches:
        fetch.start()
    barrier = pltpu.get_barrier_semaphore()
    peers = [place.device(other=True)]
    peers += [place.device(dz=d, other=flip) for d in range(1, 8) for flip in (False, True)]
    peers += [place.device(dx=d) for d in (1, 2, 3)] + [place.device(dy=d) for d in (1, 2, 3)]
    greet(barrier, peers)

    @pl.when(place.c != place.xh)
    def _():
        greet(barrier, [place.swap()])

    fetches[0].wait()

    @pl.when(place.c != place.xh)
    def _():
        pl.semaphore_wait(barrier, len(peers) + 1)

    @pl.when(place.c == place.xh)
    def _():
        pl.semaphore_wait(barrier, len(peers))

    def prepare():
        fetches[1].wait()
        fetches[2].wait()
        factors(left, right, lp, rt)

    def meanwhile():
        for fetch in fetches[3:]:
            fetch.wait()
        decode(tables, ops, code)
        widen(code, turns, wide)

    def turn_rows():
        form_rows(place.z, code, pw, wide, xp, xpt)

    gather(
        place, net, raw, pw, qw, rq, lp, rt, rown, stripe_send, stripe_recv,
        prepare, meanwhile, turn_rows,
    )
    form_screen(rq, lp, screen)
    form_columns(place, code, qw, wide, xq)
    form_density(xp, xq, density)
    mix(screen, density, mixed)
    close_and_reduce(place, net, xpt, xq, mixed, e, sib, sb, rb, sz, zb, out)
    net.finish()


VM = pl.BlockSpec(memory_space=pltpu.VMEM)
HB = pl.BlockSpec(memory_space=pl.ANY)
COPIES = 180


def body(wedge_orbitals, star_members, star_ops, rotations, screen_left, screen_right):
    sem = pltpu.SemaphoreType.DMA((COPIES,))
    return pl.pallas_call(
        kernel,
        out_shape=jax.ShapeDtypeStruct((2, 1, 8, 128), F32),
        in_specs=[HB] * 6,
        out_specs=VM,
        scratch_shapes=[
            pltpu.SMEM((4, NK), jnp.int32),
            pltpu.SMEM((4, NK), jnp.int32),
            pltpu.VMEM((STOPS, 64, 256), BF),
            pltpu.VMEM((STOPS, 64, 256), BF),
            pltpu.VMEM((2, 256, NB), BF),
            pltpu.VMEM((8, 2, 2, 256, 128), BF),
            pltpu.VMEM((2, 2, 8, 4, 2, 2, 16, 128), BF),
            pltpu.VMEM((3, 4, 2, 2, 16, 128), BF),
            pltpu.VMEM((2, 3, 256, 128), BF),
            pltpu.VMEM((3, 256, 128), BF),
            pltpu.VMEM((2, 3, 16, 128), BF),
            pltpu.SMEM((NK,), jnp.int32),
            pltpu.VMEM((48, NB, NB), BF),
            pltpu.VMEM((NK, 256, 256), BF),
            pltpu.VMEM((NK, 256, 256), BF),
            pltpu.VMEM((NK, NB, 512), BF),
            pltpu.VMEM((NK, 256, 256), BF),
            pltpu.VMEM((STOPS, 256, 256), F32),
            pltpu.VMEM((NK, 512, 256), F32),
            pltpu.VMEM((NK, 256, 512), BF),
            pltpu.VMEM((NK, 8, 2, 8, 256), F32),
            pltpu.VMEM((NK, 8, 8, 256), F32),
            pltpu.VMEM((2, 8, 8, 16, 128), BF),
            pltpu.VMEM((16, 8, 16, 128), BF),
            pltpu.VMEM((8, 16, 128), BF),
            pltpu.VMEM((8, 16, 128), BF),
            sem,
            sem,
            pltpu.SemaphoreType.DMA((8, 2)),
            pltpu.SemaphoreType.DMA((8, 2)),
            pltpu.SemaphoreType.DMA((6,)),
        ],
        compiler_params=pltpu.CompilerParams(
            collective_id=0, has_side_effects=True, vmem_limit_bytes=56 << 20
        ),
    )(
        star_members.T,
        star_ops.T,
        wedge_orbitals,
        rotations,
        jnp.swapaxes(screen_left, 1, 2),
        jnp.swapaxes(screen_right, 1, 2),
    )


def solution(mesh):
    return jax.shard_map(
        body,
        mesh=mesh,
        in_specs=(
            P(None, "ka", "pt", None),
            P(),
            P(),
            P(),
            P(None, "pt", None),
            P(None, "pt", None),
        ),
        out_specs=P(None, "ka", "pt", None),
        check_vma=False,
    )
```

```python
import math

import jax
import jax.numpy as jnp
from jax import lax
from jax.experimental import pallas as pl
from jax.experimental.pallas import tpu as pltpu
from jax.sharding import PartitionSpec as P

NB = 128
NPTS = 4096
STOPS = 6
NK = 16
BF = jnp.bfloat16
F32 = jnp.float32
MESH = pl.DeviceIdType.MESH
PLANE = tuple((i, j) for i in range(4) for j in range(4) if i or j)
ZS = (4, 3, 5, 2, 6, 1, 7)


class Place:
    def __init__(self):
        ka = lax.axis_index("ka")
        pt = lax.axis_index("pt")
        self.xh = lax.div(ka, 8)
        self.z = lax.rem(ka, 8)
        self.y = lax.div(pt, 4)
        self.xl = lax.rem(lax.div(pt, 2), 2)
        self.c = lax.rem(pt, 2)
        self.x = 2 * self.xh + self.xl

    def device(self, dx=0, dy=0, dz=0, other=False):
        x = lax.rem(self.x + dx, 4)
        y = lax.rem(self.y + dy, 4)
        z = lax.rem(self.z + dz, 8)
        c = 1 - self.c if other else self.c
        return (lax.div(x, 2) * 8 + z, y * 4 + lax.rem(x, 2) * 2 + c)

    def swap(self):
        return (self.c * 8 + self.z, self.y * 4 + self.xl * 2 + self.xh)


class Copies:
    def __init__(self, send, recv):
        self.send, self.recv, self.count, self.open = send, recv, 0, []

    def make(self, src, dst, device):
        i = self.count
        self.count += 1
        return pltpu.make_async_remote_copy(
            src_ref=src,
            dst_ref=dst,
            send_sem=self.send.at[i],
            recv_sem=self.recv.at[i],
            device_id=device,
            device_id_type=MESH,
        )

    def start(self, src, dst, device):
        copy = self.make(src, dst, device)
        copy.start()
        self.open.append(copy)
        return copy

    def finish(self):
        for copy in self.open:
            copy.wait_send()


def greet(barrier, devices):
    for device in devices:
        pl.semaphore_signal(barrier, inc=1, device_id=device, device_id_type=MESH)


def factors(left, right, lp, rt):
    for i in range(3):
        rt[i] = jnp.concatenate([right[2 * i], right[2 * i + 1]], axis=0).T
    for i in range(3):
        lp[1, i] = jnp.concatenate([left[2 * i], left[2 * i + 1]], axis=0).T


def decode(tables, ops, code):
    def look(w, words):
        for slot in range(4):
            member = tables[slot, w]
            word = w * 64 + ops[slot, w]
            words = tuple(jnp.where(member == k, word, words[k]) for k in range(NK))
        return words

    words = lax.fori_loop(0, NK, look, (jnp.int32(0),) * NK)
    for k in range(NK):
        code[k] = words[k]


def widen(code, rotations, wide):
    for k in range(NK):
        rotation = rotations[lax.rem(code[k], 64)]
        zero = jnp.zeros_like(rotation)
        wide[k] = jnp.concatenate(
            [jnp.concatenate([rotation, zero], axis=1), jnp.concatenate([zero, rotation], axis=1)],
            axis=0,
        )


def gather(
    place, net, raw, pw, qw, rq, lp, rt, rown, stripe_send, stripe_recv, prepare, meanwhile, turn_columns, turn_rows
):
    c, xh, xl, z = place.c, place.xh, place.xl, place.z
    straight = c == xh
    other = place.device(other=True)
    plus, minus = place.device(dz=1), place.device(dz=7)

    def stripe(dz, flip):
        core = 1 - c if flip else c
        row = pl.multiple_of(32 * lax.rem(z + dz, 8) + 16 * core, 16)
        return pltpu.make_async_remote_copy(
            src_ref=raw.at[:, pl.ds(row, 16), :],
            dst_ref=qw[0].at[:, 0, (8 - dz) % 8, 0, 0, c],
            send_sem=stripe_send.at[dz, flip],
            recv_sem=stripe_recv.at[dz, c],
            device_id=place.device(dz=dz, other=bool(flip)),
            device_id_type=MESH,
        )

    def stripe_arrival(dz, core):
        return pltpu.make_async_remote_copy(
            src_ref=raw.at[:, pl.ds(0, 16), :],
            dst_ref=qw[0].at[:, 0, (8 - dz) % 8, 0, 0, core],
            send_sem=stripe_send.at[dz, core],
            recv_sem=stripe_recv.at[dz, core],
            device_id=other,
            device_id_type=MESH,
        )

    for dz in ZS:
        for flip in range(2):
            stripe(dz, flip).start()
    stripe(0, 1).start()
    swap = net.make(raw, pw.at[0, xh], place.swap())
    own_row = pl.multiple_of(32 * z + 16 * c, 16)
    other_row = pl.multiple_of(32 * z + 16 * (1 - c), 16)

    @pl.when(c != xh)
    def _():
        swap.start()

    qw[0][:, 0, 0, 0, 0, c] = raw[:, pl.ds(own_row, 16), :]

    ups, downs, beside = {}, {}, {}

    def forward(step, ri):
        up, down = (8 - step) % 8, step
        if step < 3 or (step == 3 and ri == 0):
            ups[step, ri] = net.make(pw.at[up, c, ri], pw.at[up - 1 if up else 7, c, ri], plus)
        if step < 3 or (step == 3 and ri == 1):
            downs[step, ri] = net.make(pw.at[down, c, ri], pw.at[down + 1, c, ri], minus)
        return [group[step, ri] for group in (ups, downs) if (step, ri) in group]

    def share(rel, ri):
        beside[rel, ri] = net.make(pw.at[rel, c, ri], pw.at[rel, c, ri], other)
        return [beside[rel, ri]]

    def launch(copies, keep=True):
        for copy in copies:
            copy.start()
        if keep:
            net.open.extend(copies)

    first = []
    for ri in range(2):
        first += forward(0, ri)
    for ri in range(2):
        first += share(0, ri)
    net.open.extend(first)

    @pl.when(straight)
    def _():
        pw[0, c] = raw[...]
        launch(first, False)

    prepare()
    give_left = net.make(lp.at[1], lp.at[0], other)
    give_right = net.make(rown.at[1], rown.at[0], other)

    @pl.when(straight)
    def _():
        for i in range(3):
            rown[0, i] = rt[i, pl.ds(own_row, 16), :]
            rown[1, i] = rt[i, pl.ds(other_row, 16), :]
        give_right.start()
        give_left.start()
        lp[0] = lp[1]

    @pl.when(c != xh)
    def _():
        swap.wait_recv()
        launch(first, False)
        give_right.wait_recv()

    rq[:, 0, 0, xh] = rown[0]
    for dz in (0, 1, 7, 2, 6, 3, 5, 4):
        for core in range(2):
            if dz:
                stripe_arrival(dz, core).wait_recv()
    stripe_arrival(0, 1 - c).wait_recv()

    turned_x = (0, xl, 1, 1 - xl)

    def tile(h, px, py):
        return qw[py // 2].at[h, turned_x[px], :, py % 2, px % 2]

    def sent_tile(h, px, py, dx, dy):
        qx, qy = (px + 4 - dx) % 4, (py + 4 - dy) % 4
        there = lax.rem(xl + dx, 2)
        turned = (0, there, 1, 1 - there)[qx]
        return qw[qy // 2].at[h, turned, :, qy % 2, qx % 2]

    def pass_on(h, px, py, dx, dy):
        return net.start(tile(h, px, py), sent_tile(h, px, py, dx, dy), place.device(dx=dx, dy=dy))

    rows, columns, factor, rest, early, late = {}, {}, {}, [], [], []
    for d in (2, 1, 3):
        rows[d] = pass_on(0, 0, 0, d, 0)
        columns[d] = pass_on(1, 0, 0, 0, d)
    for d in (2, 1, 3):
        factor[d] = net.start(rq.at[:, 0, 0, xh], rq.at[:, 4 - d, 0, xh], place.device(dy=d))
    for d in (2, 1, 3):
        rest.append(pass_on(1, 0, 0, d, 0))
        rest.append(pass_on(0, 0, 0, 0, d))

    def ring(step):
        for ri in range(2):
            if step < 4:
                ups[step - 1, ri].wait_recv()
                downs[step - 1, ri].wait_recv()
                launch(forward(step, ri) + share(8 - step, ri) + share(step, ri))
            else:
                (ups if ri == 0 else downs)[3, ri].wait_recv()
                launch(share(4, ri))

    ring(1)
    meanwhile()
    for d in (1, 3, 2):
        factor[d].wait_recv()
    for dx in (2, 1, 3):
        early.append(
            net.start(
                rq.at[:, :, 0, xh], rq.at[:, :, (4 - dx) % 2, xh], place.device(dx=dx)
            )
        )
    for d in (1, 3, 2):
        rows[d].wait_recv()
        early.append(pass_on(0, 4 - d, 0, 0, 3))
    columns[3].wait_recv()
    for dx in (2, 1, 3):
        early.append(pass_on(1, 0, 1, dx, 0))
    for d in (1, 3, 2):
        for dy in (2, 1):
            late.append(pass_on(0, 4 - d, 0, 0, dy))
        if d != 3:
            columns[d].wait_recv()
            for dx in (2, 1, 3):
                late.append(pass_on(1, 0, 4 - d, dx, 0))
    ring(2)
    ring(3)
    ring(4)
    for copy in rest + early:
        copy.wait_recv()

    @pl.when(c != xh)
    def _():
        give_left.wait_recv()

    turn_columns()
    for copy in beside.values():
        copy.wait_recv()
    turn_rows()
    for copy in late:
        copy.wait_recv()

    @pl.when(c != xh)
    def _():
        swap.wait_send()

    @pl.when(straight)
    def _():
        give_right.wait_send()
        give_left.wait_send()

    for dz in ZS:
        for flip in range(2):
            stripe(dz, flip).wait_send()
    stripe(0, 1).wait_send()


def dot(a, b, ca, cb):
    return lax.dot_general(a, b, (((ca,), (cb,)), ((), ())), preferred_element_type=F32)


def form_screen(half, rq, lp, screen):
    lane = lax.broadcasted_iota(jnp.int32, (256, 128), 1)
    columns = slice(half * 128, half * 128 + 128)
    for i in range(3):
        factor = rq[i, 2 * half : 2 * half + 2].reshape(128, 128)
        rows = lp[0, i]
        zero = jnp.zeros_like(rows)
        screen[2 * i, :, columns] = dot(jnp.where(lane < 64, rows, zero), factor, 1, 1)
        screen[2 * i + 1, :, columns] = dot(jnp.where(lane < 64, zero, rows), factor, 1, 1)


def seat(z, word):
    w = lax.div(word, 64)
    return lax.div(w, 8), lax.rem(lax.rem(w, 8) - z + 8, 8)


def form_rows(z, code, pw, wide, xp, xpt):
    for k in range(NK):
        u, rel = seat(z, code[k])
        raw = jnp.concatenate([pw[rel, u, 0], pw[rel, u, 1]], axis=1)
        turned = dot(raw, wide[k], 1, 0).astype(BF)
        xp[k] = turned
        xpt[k] = jnp.concatenate([turned[:, :128], turned[:, 128:]], axis=0).T


def form_columns(half, place, code, qw, wide, xq):
    for k in range(NK):
        u, rel = seat(place.z, code[k])
        turned = jnp.where(u == place.xh, 0, 1)
        raw = jnp.concatenate(
            [
                qw[half][0, turned, rel].reshape(128, 128),
                qw[half][1, turned, rel].reshape(128, 128),
            ],
            axis=1,
        )
        xq[k, half * 128 : half * 128 + 128] = dot(raw, wide[k], 1, 0).astype(BF)


def form_density(half, xp, xq, density):
    columns = slice(half * 128, half * 128 + 128)
    for k in range(NK):
        rows = xp[k]
        stacked = jnp.concatenate(
            [rows, jnp.concatenate([rows[:, 128:], -rows[:, :128]], axis=1)], axis=0
        )
        density[k, :, columns] = dot(stacked, xq[k, columns], 1, 1)


def mix(half, ks, screen, density, mixed):
    columns = pl.ds(half * 128, 128)

    def step(t, carry):
        top = pl.multiple_of(t * 16, 16)
        s = [screen[i, pl.ds(top, 16), columns] for i in range(STOPS)]
        for part in range(2):
            source = pl.multiple_of(part * 256 + top, 16)
            d = [density[j, pl.ds(source, 16), columns] for j in range(NK)]
            for k in ks:
                total = d[(k + 3) % NK] * s[0]
                for i in range(1, STOPS):
                    total = total + d[(k + 3 - i) % NK] * s[i]
                mixed[k, pl.ds(top, 16), pl.ds(part * 256 + half * 128, 128)] = total.astype(BF)
        return carry

    lax.fori_loop(0, 16, step, 0)


def close(ks, xpt, xq, mixed, e):
    ys = []
    for k in ks:
        q = xq[k]
        operand = jnp.concatenate(
            [q, jnp.concatenate([-q[:, 128:], q[:, :128]], axis=1)], axis=0
        )
        ys.append(dot(mixed[k], operand, 1, 0).astype(BF))
    for k, y in zip(ks, ys):
        turned = jnp.concatenate([y, jnp.concatenate([y[:, 128:], -y[:, :128]], axis=1)], axis=0)
        e[k] = dot(xpt[k], turned, 1, 0).reshape(8, 2, 8, 256)


def close_and_reduce(place, net, screen, density, xpt, xq, mixed, e, sib, sb, rb, sz, zb, out):
    c, x, y, z, xh, xl = place.c, place.x, place.y, place.z, place.xh, place.xl
    other = place.device(other=True)

    def batch(b):
        return [8 * h + b * SIZE + i for h in range(2) for i in range(SIZE)]

    def hand(b):
        copies = []
        for h in range(2):
            ks = pl.ds(8 * h + b * SIZE, SIZE)
            copies.append(net.start(e.at[ks, :, 1 - c], sib.at[ks], other))
        return copies

    def fold(b, copies):
        for h in range(2):
            copies[h].wait_recv()
            for i in range(b * SIZE, (b + 1) * SIZE):
                value = e[8 * h + i, :, c] + sib[8 * h + i]
                value = jnp.concatenate([value[:, :, :128], value[:, :, 128:]], axis=1)
                sb[h, :, i] = value.astype(BF)

    def scatter(b):
        copies = []
        zz = pl.ds(b * SIZE, SIZE)
        for dx, dy in FAR_FIRST:
            tx = lax.rem(x + dx, 4)
            ty = lax.rem(y + dy, 4)
            copies.append(
                net.start(
                    sb.at[lax.div(tx, 2), ty * 2 + lax.rem(tx, 2), zz],
                    rb.at[dx * 4 + dy, zz],
                    place.device(dx=dx, dy=dy),
                )
            )
        return copies

    def collect(b, copies):
        zz = pl.ds(b * SIZE, SIZE)
        total = sb[xh, y * 2 + xl, zz].astype(F32)
        for (dx, dy), copy in zip(reversed(FAR_FIRST), reversed(copies)):
            copy.wait_recv()
            total = total + rb[dx * 4 + dy, zz].astype(F32)
        sz[zz] = total.astype(BF)

    handed, sent = {}, {}
    for b in range(BATCHES):
        ks = batch(b)
        mix(1, ks, screen, density, mixed)
        if b:
            fold(b - 1, handed[b - 1])
            sent[b - 1] = scatter(b - 1)
        close(ks, xpt, xq, mixed, e)
        handed[b] = hand(b)
    fold(BATCHES - 1, handed[BATCHES - 1])
    sent[BATCHES - 1] = scatter(BATCHES - 1)
    for b in range(BATCHES):
        collect(b, sent[b])
    last = []
    for dz in ZS:
        last.append(net.start(sz.at[lax.rem(z + dz, 8)], zb.at[dz], place.device(dz=dz)))
    value = sz[z].astype(F32)
    for dz, copy in zip(ZS, last):
        copy.wait_recv()
        value = value + zb[dz].astype(F32)
    value = value * (1.0 / (4.0 * NPTS * math.sqrt(NB)))
    out[0, 0] = value[:8]
    out[1, 0] = value[8:]


FAR_FIRST = tuple(sorted(PLANE, key=lambda d: -min(d[0], 4 - d[0]) - min(d[1], 4 - d[1])))
BATCHES = 2
SIZE = 8 // BATCHES


def kernel(
    star, star_op, wedge, rotations, screen_left, screen_right, out,
    tables, ops, left, right, raw, pw, qw_near, qw_far, rq, lp, rt, rown, code, turns, wide, xp, xpt, xq, screen,
    density, mixed, e, sib, sb, rb, sz, zb, send, recv, stripe_send, stripe_recv, local,
):
    place = Place()
    net = Copies(send, recv)
    qw = (qw_near, qw_far)
    fetches = [
        pltpu.make_async_copy(source, target, local.at[i])
        for i, (source, target) in enumerate(
            (
                (wedge.at[:, 0], raw),
                (screen_right, right),
                (screen_left, left),
                (star, tables),
                (star_op, ops),
                (rotations, turns),
            )
        )
    ]
    for fetch in fetches:
        fetch.start()
    barrier = pltpu.get_barrier_semaphore()
    peers = [place.device(other=True)]
    peers += [place.device(dz=d, other=flip) for d in range(1, 8) for flip in (False, True)]
    peers += [place.device(dx=d) for d in (1, 2, 3)] + [place.device(dy=d) for d in (1, 2, 3)]
    greet(barrier, peers)

    @pl.when(place.c != place.xh)
    def _():
        greet(barrier, [place.swap()])

    fetches[0].wait()

    @pl.when(place.c != place.xh)
    def _():
        pl.semaphore_wait(barrier, len(peers) + 1)

    @pl.when(place.c == place.xh)
    def _():
        pl.semaphore_wait(barrier, len(peers))

    def prepare():
        fetches[1].wait()
        fetches[2].wait()
        factors(left, right, lp, rt)

    def meanwhile():
        for fetch in fetches[3:]:
            fetch.wait()
        decode(tables, ops, code)
        widen(code, turns, wide)

    def turn_columns():
        form_screen(0, rq, lp, screen)
        form_columns(0, place, code, qw, wide, xq)

    def turn_rows():
        form_rows(place.z, code, pw, wide, xp, xpt)
        form_density(0, xp, xq, density)
        mix(0, range(NK), screen, density, mixed)

    gather(
        place, net, raw, pw, qw, rq, lp, rt, rown, stripe_send, stripe_recv,
        prepare, meanwhile, turn_columns, turn_rows,
    )
    form_screen(1, rq, lp, screen)
    form_columns(1, place, code, qw, wide, xq)
    form_density(1, xp, xq, density)
    close_and_reduce(place, net, screen, density, xpt, xq, mixed, e, sib, sb, rb, sz, zb, out)
    net.finish()


VM = pl.BlockSpec(memory_space=pltpu.VMEM)
HB = pl.BlockSpec(memory_space=pl.ANY)
COPIES = 180


def body(wedge_orbitals, star_members, star_ops, rotations, screen_left, screen_right):
    sem = pltpu.SemaphoreType.DMA((COPIES,))
    return pl.pallas_call(
        kernel,
        out_shape=jax.ShapeDtypeStruct((2, 1, 8, 128), F32),
        in_specs=[HB] * 6,
        out_specs=VM,
        scratch_shapes=[
            pltpu.SMEM((4, NK), jnp.int32),
            pltpu.SMEM((4, NK), jnp.int32),
            pltpu.VMEM((STOPS, 64, 256), BF),
            pltpu.VMEM((STOPS, 64, 256), BF),
            pltpu.VMEM((2, 256, NB), BF),
            pltpu.VMEM((8, 2, 2, 256, 128), BF),
            pltpu.VMEM((2, 2, 8, 2, 2, 2, 16, 128), BF),
            pltpu.VMEM((2, 2, 8, 2, 2, 2, 16, 128), BF),
            pltpu.VMEM((3, 4, 2, 2, 16, 128), BF),
            pltpu.VMEM((2, 3, 256, 128), BF),
            pltpu.VMEM((3, 256, 128), BF),
            pltpu.VMEM((2, 3, 16, 128), BF),
            pltpu.SMEM((NK,), jnp.int32),
            pltpu.VMEM((48, NB, NB), BF),
            pltpu.VMEM((NK, 256, 256), BF),
            pltpu.VMEM((NK, 256, 256), BF),
            pltpu.VMEM((NK, NB, 512), BF),
            pltpu.VMEM((NK, 256, 256), BF),
            pltpu.VMEM((STOPS, 256, 256), F32),
            pltpu.VMEM((NK, 512, 256), F32),
            pltpu.VMEM((NK, 256, 512), BF),
            pltpu.VMEM((NK, 8, 2, 8, 256), F32),
            pltpu.VMEM((NK, 8, 8, 256), F32),
            pltpu.VMEM((2, 8, 8, 16, 128), BF),
            pltpu.VMEM((16, 8, 16, 128), BF),
            pltpu.VMEM((8, 16, 128), BF),
            pltpu.VMEM((8, 16, 128), BF),
            sem,
            sem,
            pltpu.SemaphoreType.DMA((8, 2)),
            pltpu.SemaphoreType.DMA((8, 2)),
            pltpu.SemaphoreType.DMA((6,)),
        ],
        compiler_params=pltpu.CompilerParams(
            collective_id=0, has_side_effects=True, vmem_limit_bytes=56 << 20
        ),
    )(
        star_members.T,
        star_ops.T,
        wedge_orbitals,
        rotations,
        jnp.swapaxes(screen_left, 1, 2),
        jnp.swapaxes(screen_right, 1, 2),
    )


def solution(mesh):
    return jax.shard_map(
        body,
        mesh=mesh,
        in_specs=(
            P(None, "ka", "pt", None),
            P(),
            P(),
            P(),
            P(None, "pt", None),
            P(None, "pt", None),
        ),
        out_specs=P(None, "ka", "pt", None),
        check_vma=False,
    )
```

```python
import math

import jax
import jax.numpy as jnp
from jax import lax
from jax.experimental import pallas as pl
from jax.experimental.pallas import tpu as pltpu
from jax.sharding import PartitionSpec as P

NB = 128
NPTS = 4096
STOPS = 6
NK = 16
BF = jnp.bfloat16
F32 = jnp.float32
MESH = pl.DeviceIdType.MESH
PLANE = tuple((i, j) for i in range(4) for j in range(4) if i or j)
ZS = (4, 3, 5, 2, 6, 1, 7)


class Place:
    def __init__(self):
        ka = lax.axis_index("ka")
        pt = lax.axis_index("pt")
        self.xh = lax.div(ka, 8)
        self.z = lax.rem(ka, 8)
        self.y = lax.div(pt, 4)
        self.xl = lax.rem(lax.div(pt, 2), 2)
        self.c = lax.rem(pt, 2)
        self.x = 2 * self.xh + self.xl

    def device(self, dx=0, dy=0, dz=0, other=False):
        x = lax.rem(self.x + dx, 4)
        y = lax.rem(self.y + dy, 4)
        z = lax.rem(self.z + dz, 8)
        c = 1 - self.c if other else self.c
        return (lax.div(x, 2) * 8 + z, y * 4 + lax.rem(x, 2) * 2 + c)

    def swap(self):
        return (self.c * 8 + self.z, self.y * 4 + self.xl * 2 + self.xh)


class Copies:
    def __init__(self, send, recv):
        self.send, self.recv, self.count, self.open = send, recv, 0, []

    def make(self, src, dst, device):
        i = self.count
        self.count += 1
        return pltpu.make_async_remote_copy(
            src_ref=src,
            dst_ref=dst,
            send_sem=self.send.at[i],
            recv_sem=self.recv.at[i],
            device_id=device,
            device_id_type=MESH,
        )

    def start(self, src, dst, device):
        copy = self.make(src, dst, device)
        copy.start()
        self.open.append(copy)
        return copy

    def finish(self):
        for copy in self.open:
            copy.wait_send()


def greet(barrier, devices):
    for device in devices:
        pl.semaphore_signal(barrier, inc=1, device_id=device, device_id_type=MESH)


def factors(left, right, lp, rt):
    for i in range(3):
        rt[i] = jnp.concatenate([right[2 * i], right[2 * i + 1]], axis=0).T
    for i in range(3):
        lp[1, i] = jnp.concatenate([left[2 * i], left[2 * i + 1]], axis=0).T


def decode(tables, ops, code):
    def look(w, words):
        for slot in range(4):
            member = tables[slot, w]
            word = w * 64 + ops[slot, w]
            words = tuple(jnp.where(member == k, word, words[k]) for k in range(NK))
        return words

    words = lax.fori_loop(0, NK, look, (jnp.int32(0),) * NK)
    for k in range(NK):
        code[k] = words[k]


def widen(code, rotations, wide):
    for k in range(NK):
        rotation = rotations[lax.rem(code[k], 64)]
        zero = jnp.zeros_like(rotation)
        wide[k] = jnp.concatenate(
            [jnp.concatenate([rotation, zero], axis=1), jnp.concatenate([zero, rotation], axis=1)],
            axis=0,
        )


def gather(
    place, net, raw, pw, qw, rq, lp, rt, rown, stripe_send, stripe_recv, prepare, meanwhile, turn_columns, turn_rows
):
    c, xh, xl, z = place.c, place.xh, place.xl, place.z
    straight = c == xh
    other = place.device(other=True)
    plus, minus = place.device(dz=1), place.device(dz=7)

    def stripe(dz, flip):
        core = 1 - c if flip else c
        row = pl.multiple_of(32 * lax.rem(z + dz, 8) + 16 * core, 16)
        return pltpu.make_async_remote_copy(
            src_ref=raw.at[:, pl.ds(row, 16), :],
            dst_ref=qw[0].at[:, 0, (8 - dz) % 8, 0, 0, c],
            send_sem=stripe_send.at[dz, flip],
            recv_sem=stripe_recv.at[dz, c],
            device_id=place.device(dz=dz, other=bool(flip)),
            device_id_type=MESH,
        )

    def stripe_arrival(dz, core):
        return pltpu.make_async_remote_copy(
            src_ref=raw.at[:, pl.ds(0, 16), :],
            dst_ref=qw[0].at[:, 0, (8 - dz) % 8, 0, 0, core],
            send_sem=stripe_send.at[dz, core],
            recv_sem=stripe_recv.at[dz, core],
            device_id=other,
            device_id_type=MESH,
        )

    swap = net.make(raw, pw.at[0, xh], place.swap())
    own_row = pl.multiple_of(32 * z + 16 * c, 16)
    other_row = pl.multiple_of(32 * z + 16 * (1 - c), 16)

    @pl.when(c != xh)
    def _():
        swap.start()

    for dz in ZS:
        for flip in range(2):
            stripe(dz, flip).start()
    stripe(0, 1).start()
    qw[0][:, 0, 0, 0, 0, c] = raw[:, pl.ds(own_row, 16), :]

    ups, downs, beside = {}, {}, {}

    def forward(step, ri):
        up, down = (8 - step) % 8, step
        if step < 3 or (step == 3 and ri == 0):
            ups[step, ri] = net.make(pw.at[up, c, ri], pw.at[up - 1 if up else 7, c, ri], plus)
        if step < 3 or (step == 3 and ri == 1):
            downs[step, ri] = net.make(pw.at[down, c, ri], pw.at[down + 1, c, ri], minus)
        return [group[step, ri] for group in (ups, downs) if (step, ri) in group]

    def share(rel, ri):
        beside[rel, ri] = net.make(pw.at[rel, c, ri], pw.at[rel, c, ri], other)
        return [beside[rel, ri]]

    def launch(copies, keep=True):
        for copy in copies:
            copy.start()
        if keep:
            net.open.extend(copies)

    first = []
    for ri in range(2):
        first += forward(0, ri)
    for ri in range(2):
        first += share(0, ri)
    net.open.extend(first)

    @pl.when(straight)
    def _():
        pw[0, c] = raw[...]
        launch(first, False)

    prepare()
    give_left = net.make(lp.at[1], lp.at[0], other)
    give_right = net.make(rown.at[1], rown.at[0], other)

    @pl.when(straight)
    def _():
        for i in range(3):
            rown[0, i] = rt[i, pl.ds(own_row, 16), :]
            rown[1, i] = rt[i, pl.ds(other_row, 16), :]
        give_right.start()
        give_left.start()
        lp[0] = lp[1]

    @pl.when(c != xh)
    def _():
        swap.wait_recv()
        launch(first, False)
        give_right.wait_recv()

    rq[:, 0, 0, xh] = rown[0]
    for dz in (0, 1, 7, 2, 6, 3, 5, 4):
        for core in range(2):
            if dz:
                stripe_arrival(dz, core).wait_recv()
    stripe_arrival(0, 1 - c).wait_recv()

    turned_x = (0, xl, 1, 1 - xl)

    def tile(h, px, py):
        return qw[py // 2].at[h, turned_x[px], :, py % 2, px % 2]

    def sent_tile(h, px, py, dx, dy):
        qx, qy = (px + 4 - dx) % 4, (py + 4 - dy) % 4
        there = lax.rem(xl + dx, 2)
        turned = (0, there, 1, 1 - there)[qx]
        return qw[qy // 2].at[h, turned, :, qy % 2, qx % 2]

    def pass_on(h, px, py, dx, dy):
        return net.start(tile(h, px, py), sent_tile(h, px, py, dx, dy), place.device(dx=dx, dy=dy))

    rows, columns, factor, rest, early, late = {}, {}, {}, [], [], []
    for d in (2, 1, 3):
        rows[d] = pass_on(0, 0, 0, d, 0)
        columns[d] = pass_on(1, 0, 0, 0, d)
    for d in (2, 1, 3):
        factor[d] = net.start(rq.at[:, 0, 0, xh], rq.at[:, 4 - d, 0, xh], place.device(dy=d))
    for d in (2, 1, 3):
        rest.append(pass_on(1, 0, 0, d, 0))
        rest.append(pass_on(0, 0, 0, 0, d))

    def ring(step):
        for ri in range(2):
            if step < 4:
                ups[step - 1, ri].wait_recv()
                downs[step - 1, ri].wait_recv()
                launch(forward(step, ri) + share(8 - step, ri) + share(step, ri))
            else:
                (ups if ri == 0 else downs)[3, ri].wait_recv()
                launch(share(4, ri))

    ring(1)
    meanwhile()
    for d in (1, 3, 2):
        factor[d].wait_recv()
    for dx in (2, 1, 3):
        early.append(
            net.start(
                rq.at[:, :, 0, xh], rq.at[:, :, (4 - dx) % 2, xh], place.device(dx=dx)
            )
        )
    for d in (1, 3, 2):
        rows[d].wait_recv()
        early.append(pass_on(0, 4 - d, 0, 0, 3))
    columns[3].wait_recv()
    for dx in (2, 1, 3):
        early.append(pass_on(1, 0, 1, dx, 0))
    for d in (1, 3, 2):
        for dy in (2, 1):
            late.append(pass_on(0, 4 - d, 0, 0, dy))
        if d != 3:
            columns[d].wait_recv()
            for dx in (2, 1, 3):
                late.append(pass_on(1, 0, 4 - d, dx, 0))
    ring(2)
    ring(3)
    ring(4)
    for copy in rest + early:
        copy.wait_recv()

    @pl.when(c != xh)
    def _():
        give_left.wait_recv()

    turn_columns()
    for copy in beside.values():
        copy.wait_recv()
    turn_rows()
    for copy in late:
        copy.wait_recv()

    @pl.when(c != xh)
    def _():
        swap.wait_send()

    @pl.when(straight)
    def _():
        give_right.wait_send()
        give_left.wait_send()

    for dz in ZS:
        for flip in range(2):
            stripe(dz, flip).wait_send()
    stripe(0, 1).wait_send()


def dot(a, b, ca, cb):
    return lax.dot_general(a, b, (((ca,), (cb,)), ((), ())), preferred_element_type=F32)


def form_screen(half, rq, lp, screen):
    lane = lax.broadcasted_iota(jnp.int32, (256, 128), 1)
    columns = slice(half * 128, half * 128 + 128)
    for i in range(3):
        factor = rq[i, 2 * half : 2 * half + 2].reshape(128, 128)
        rows = lp[0, i]
        zero = jnp.zeros_like(rows)
        screen[2 * i, :, columns] = dot(jnp.where(lane < 64, rows, zero), factor, 1, 1)
        screen[2 * i + 1, :, columns] = dot(jnp.where(lane < 64, zero, rows), factor, 1, 1)


def seat(z, word):
    w = lax.div(word, 64)
    return lax.div(w, 8), lax.rem(lax.rem(w, 8) - z + 8, 8)


def form_rows(z, code, pw, wide, xp, xpt):
    for k in range(NK):
        u, rel = seat(z, code[k])
        raw = jnp.concatenate([pw[rel, u, 0], pw[rel, u, 1]], axis=1)
        turned = dot(raw, wide[k], 1, 0).astype(BF)
        xp[k] = turned
        xpt[k] = jnp.concatenate([turned[:, :128], turned[:, 128:]], axis=0).T


def form_columns(half, place, code, qw, wide, xq):
    for k in range(NK):
        u, rel = seat(place.z, code[k])
        turned = jnp.where(u == place.xh, 0, 1)
        raw = jnp.concatenate(
            [
                qw[half][0, turned, rel].reshape(128, 128),
                qw[half][1, turned, rel].reshape(128, 128),
            ],
            axis=1,
        )
        xq[k, half * 128 : half * 128 + 128] = dot(raw, wide[k], 1, 0).astype(BF)


def form_density(half, xp, xq, density):
    columns = slice(half * 128, half * 128 + 128)
    for k in range(NK):
        rows = xp[k]
        stacked = jnp.concatenate(
            [rows, jnp.concatenate([rows[:, 128:], -rows[:, :128]], axis=1)], axis=0
        )
        density[k, :, columns] = dot(stacked, xq[k, columns], 1, 1)


def mix(half, ks, screen, density, mixed):
    columns = pl.ds(half * 128, 128)

    def step(t, carry):
        top = pl.multiple_of(t * 16, 16)
        s = [screen[i, pl.ds(top, 16), columns] for i in range(STOPS)]
        for part in range(2):
            source = pl.multiple_of(part * 256 + top, 16)
            d = [density[j, pl.ds(source, 16), columns] for j in range(NK)]
            for k in ks:
                total = d[(k + 3) % NK] * s[0]
                for i in range(1, STOPS):
                    total = total + d[(k + 3 - i) % NK] * s[i]
                mixed[k, pl.ds(top, 16), pl.ds(part * 256 + half * 128, 128)] = total.astype(BF)
        return carry

    lax.fori_loop(0, 16, step, 0, unroll=4)


def close(ks, xpt, xq, mixed, e):
    ys = []
    for k in ks:
        q = xq[k]
        operand = jnp.concatenate(
            [q, jnp.concatenate([-q[:, 128:], q[:, :128]], axis=1)], axis=0
        )
        ys.append(dot(mixed[k], operand, 1, 0).astype(BF))
    for k, y in zip(ks, ys):
        turned = jnp.concatenate([y, jnp.concatenate([y[:, 128:], -y[:, :128]], axis=1)], axis=0)
        e[k] = dot(xpt[k], turned, 1, 0).reshape(8, 2, 8, 256)


def close_and_reduce(place, net, screen, density, xpt, xq, mixed, e, sib, sb, rb, sz, zb, out):
    c, x, y, z, xh, xl = place.c, place.x, place.y, place.z, place.xh, place.xl
    other = place.device(other=True)

    def batch(b):
        return [8 * h + b * SIZE + i for h in range(2) for i in range(SIZE)]

    def hand(first):
        ks = pl.ds(first, SIZE)
        return net.start(e.at[ks, :, 1 - c], sib.at[ks], other)

    def fold(b, copies):
        for h in range(2):
            copies[h].wait_recv()
            for i in range(b * SIZE, (b + 1) * SIZE):
                value = e[8 * h + i, :, c] + sib[8 * h + i]
                value = jnp.concatenate([value[:, :, :128], value[:, :, 128:]], axis=1)
                sb[h, :, i] = value.astype(BF)

    def scatter(b):
        copies = []
        zz = pl.ds(b * SIZE, SIZE)
        for dx, dy in FAR_FIRST:
            tx = lax.rem(x + dx, 4)
            ty = lax.rem(y + dy, 4)
            copies.append(
                net.start(
                    sb.at[lax.div(tx, 2), ty * 2 + lax.rem(tx, 2), zz],
                    rb.at[dx * 4 + dy, zz],
                    place.device(dx=dx, dy=dy),
                )
            )
        return copies

    def collect(b, copies):
        zz = pl.ds(b * SIZE, SIZE)
        total = sb[xh, y * 2 + xl, zz].astype(F32)
        for (dx, dy), copy in zip(reversed(FAR_FIRST), reversed(copies)):
            copy.wait_recv()
            total = total + rb[dx * 4 + dy, zz].astype(F32)
        sz[zz] = total.astype(BF)

    handed, sent = {}, {}
    for b in range(BATCHES):
        ks = batch(b)
        mix(1, ks, screen, density, mixed)
        if b:
            fold(b - 1, handed[b - 1])
            sent[b - 1] = scatter(b - 1)
        handed[b] = []
        for h in range(2):
            close(ks[h * SIZE : h * SIZE + SIZE], xpt, xq, mixed, e)
            handed[b].append(hand(8 * h + b * SIZE))
    fold(BATCHES - 1, handed[BATCHES - 1])
    sent[BATCHES - 1] = scatter(BATCHES - 1)
    for b in range(BATCHES):
        collect(b, sent[b])
    last = []
    for dz in ZS:
        last.append(net.start(sz.at[lax.rem(z + dz, 8)], zb.at[dz], place.device(dz=dz)))
    value = sz[z].astype(F32)
    for dz, copy in zip(ZS, last):
        copy.wait_recv()
        value = value + zb[dz].astype(F32)
    value = value * (1.0 / (4.0 * NPTS * math.sqrt(NB)))
    out[0, 0] = value[:8]
    out[1, 0] = value[8:]


FAR_FIRST = tuple(sorted(PLANE, key=lambda d: -min(d[0], 4 - d[0]) - min(d[1], 4 - d[1])))
BATCHES = 2
SIZE = 8 // BATCHES


def kernel(
    star, star_op, wedge, rotations, screen_left, screen_right, out,
    tables, ops, left, right, raw, pw, qw_near, qw_far, rq, lp, rt, rown, code, turns, wide, xp, xpt, xq, screen,
    density, mixed, e, sib, sb, rb, sz, zb, send, recv, stripe_send, stripe_recv, local,
):
    place = Place()
    net = Copies(send, recv)
    qw = (qw_near, qw_far)
    fetches = [
        pltpu.make_async_copy(source, target, local.at[i])
        for i, (source, target) in enumerate(
            (
                (wedge.at[:, 0], raw),
                (screen_right, right),
                (screen_left, left),
                (star, tables),
                (star_op, ops),
                (rotations, turns),
            )
        )
    ]
    for fetch in fetches:
        fetch.start()
    barrier = pltpu.get_barrier_semaphore()
    peers = [place.device(other=True)]
    peers += [place.device(dz=d, other=flip) for d in range(1, 8) for flip in (False, True)]
    peers += [place.device(dx=d) for d in (1, 2, 3)] + [place.device(dy=d) for d in (1, 2, 3)]
    greet(barrier, peers)

    @pl.when(place.c != place.xh)
    def _():
        greet(barrier, [place.swap()])

    fetches[0].wait()

    @pl.when(place.c != place.xh)
    def _():
        pl.semaphore_wait(barrier, len(peers) + 1)

    @pl.when(place.c == place.xh)
    def _():
        pl.semaphore_wait(barrier, len(peers))

    def prepare():
        fetches[1].wait()
        fetches[2].wait()
        factors(left, right, lp, rt)

    def meanwhile():
        for fetch in fetches[3:]:
            fetch.wait()
        decode(tables, ops, code)
        widen(code, turns, wide)

    def turn_columns():
        form_screen(0, rq, lp, screen)
        form_columns(0, place, code, qw, wide, xq)

    def turn_rows():
        form_rows(place.z, code, pw, wide, xp, xpt)
        form_density(0, xp, xq, density)
        mix(0, range(NK), screen, density, mixed)

    gather(
        place, net, raw, pw, qw, rq, lp, rt, rown, stripe_send, stripe_recv,
        prepare, meanwhile, turn_columns, turn_rows,
    )
    form_screen(1, rq, lp, screen)
    form_columns(1, place, code, qw, wide, xq)
    form_density(1, xp, xq, density)
    close_and_reduce(place, net, screen, density, xpt, xq, mixed, e, sib, sb, rb, sz, zb, out)
    net.finish()


VM = pl.BlockSpec(memory_space=pltpu.VMEM)
HB = pl.BlockSpec(memory_space=pl.ANY)
COPIES = 180


def body(wedge_orbitals, star_members, star_ops, rotations, screen_left, screen_right):
    sem = pltpu.SemaphoreType.DMA((COPIES,))
    return pl.pallas_call(
        kernel,
        out_shape=jax.ShapeDtypeStruct((2, 1, 8, 128), F32),
        in_specs=[HB] * 6,
        out_specs=VM,
        scratch_shapes=[
            pltpu.SMEM((4, NK), jnp.int32),
            pltpu.SMEM((4, NK), jnp.int32),
            pltpu.VMEM((STOPS, 64, 256), BF),
            pltpu.VMEM((STOPS, 64, 256), BF),
            pltpu.VMEM((2, 256, NB), BF),
            pltpu.VMEM((8, 2, 2, 256, 128), BF),
            pltpu.VMEM((2, 2, 8, 2, 2, 2, 16, 128), BF),
            pltpu.VMEM((2, 2, 8, 2, 2, 2, 16, 128), BF),
            pltpu.VMEM((3, 4, 2, 2, 16, 128), BF),
            pltpu.VMEM((2, 3, 256, 128), BF),
            pltpu.VMEM((3, 256, 128), BF),
            pltpu.VMEM((2, 3, 16, 128), BF),
            pltpu.SMEM((NK,), jnp.int32),
            pltpu.VMEM((48, NB, NB), BF),
            pltpu.VMEM((NK, 256, 256), BF),
            pltpu.VMEM((NK, 256, 256), BF),
            pltpu.VMEM((NK, NB, 512), BF),
            pltpu.VMEM((NK, 256, 256), BF),
            pltpu.VMEM((STOPS, 256, 256), F32),
            pltpu.VMEM((NK, 512, 256), F32),
            pltpu.VMEM((NK, 256, 512), BF),
            pltpu.VMEM((NK, 8, 2, 8, 256), F32),
            pltpu.VMEM((NK, 8, 8, 256), F32),
            pltpu.VMEM((2, 8, 8, 16, 128), BF),
            pltpu.VMEM((16, 8, 16, 128), BF),
            pltpu.VMEM((8, 16, 128), BF),
            pltpu.VMEM((8, 16, 128), BF),
            sem,
            sem,
            pltpu.SemaphoreType.DMA((8, 2)),
            pltpu.SemaphoreType.DMA((8, 2)),
            pltpu.SemaphoreType.DMA((6,)),
        ],
        compiler_params=pltpu.CompilerParams(
            collective_id=0, has_side_effects=True, vmem_limit_bytes=56 << 20
        ),
    )(
        star_members.T,
        star_ops.T,
        wedge_orbitals,
        rotations,
        jnp.swapaxes(screen_left, 1, 2),
        jnp.swapaxes(screen_right, 1, 2),
    )


def solution(mesh):
    return jax.shard_map(
        body,
        mesh=mesh,
        in_specs=(
            P(None, "ka", "pt", None),
            P(),
            P(),
            P(),
            P(None, "pt", None),
            P(None, "pt", None),
        ),
        out_specs=P(None, "ka", "pt", None),
        check_vma=False,
    )
```

```python
import math

import jax
import jax.numpy as jnp
from jax import lax
from jax.experimental import pallas as pl
from jax.experimental.pallas import tpu as pltpu
from jax.sharding import PartitionSpec as P

NB = 128
NPTS = 4096
STOPS = 6
NK = 16
BF = jnp.bfloat16
F32 = jnp.float32
MESH = pl.DeviceIdType.MESH
PLANE = tuple((i, j) for i in range(4) for j in range(4) if i or j)
ZS = (4, 3, 5, 2, 6, 1, 7)


class Place:
    def __init__(self):
        ka = lax.axis_index("ka")
        pt = lax.axis_index("pt")
        self.xh = lax.div(ka, 8)
        self.z = lax.rem(ka, 8)
        self.y = lax.div(pt, 4)
        self.xl = lax.rem(lax.div(pt, 2), 2)
        self.c = lax.rem(pt, 2)
        self.x = 2 * self.xh + self.xl

    def device(self, dx=0, dy=0, dz=0, other=False):
        x = lax.rem(self.x + dx, 4)
        y = lax.rem(self.y + dy, 4)
        z = lax.rem(self.z + dz, 8)
        c = 1 - self.c if other else self.c
        return (lax.div(x, 2) * 8 + z, y * 4 + lax.rem(x, 2) * 2 + c)

    def swap(self):
        return (self.c * 8 + self.z, self.y * 4 + self.xl * 2 + self.xh)


class Copies:
    def __init__(self, send, recv):
        self.send, self.recv, self.count, self.open = send, recv, 0, []

    def make(self, src, dst, device):
        i = self.count
        self.count += 1
        return pltpu.make_async_remote_copy(
            src_ref=src,
            dst_ref=dst,
            send_sem=self.send.at[i],
            recv_sem=self.recv.at[i],
            device_id=device,
            device_id_type=MESH,
        )

    def start(self, src, dst, device):
        copy = self.make(src, dst, device)
        copy.start()
        self.open.append(copy)
        return copy

    def finish(self):
        for copy in self.open:
            copy.wait_send()


def greet(barrier, devices):
    for device in devices:
        pl.semaphore_signal(barrier, inc=1, device_id=device, device_id_type=MESH)


def factors(left, right, lp, rt):
    for i in range(3):
        rt[i] = jnp.concatenate([right[2 * i], right[2 * i + 1]], axis=0).T
    for i in range(3):
        lp[1, i] = jnp.concatenate([left[2 * i], left[2 * i + 1]], axis=0).T


def decode(tables, ops, code):
    def look(w, words):
        for slot in range(4):
            member = tables[slot, w]
            word = w * 64 + ops[slot, w]
            words = tuple(jnp.where(member == k, word, words[k]) for k in range(NK))
        return words

    words = lax.fori_loop(0, NK, look, (jnp.int32(0),) * NK)
    for k in range(NK):
        code[k] = words[k]


def widen(code, rotations, wide):
    for k in range(NK):
        rotation = rotations[lax.rem(code[k], 64)]
        zero = jnp.zeros_like(rotation)
        wide[k] = jnp.concatenate(
            [jnp.concatenate([rotation, zero], axis=1), jnp.concatenate([zero, rotation], axis=1)],
            axis=0,
        )


def gather(
    place, net, raw, pw, qw, rq, lp, rt, rown, stripe_send, stripe_recv, prepare, meanwhile, turn_columns, turn_rows
):
    c, xh, xl, z = place.c, place.xh, place.xl, place.z
    straight = c == xh
    other = place.device(other=True)
    plus, minus = place.device(dz=1), place.device(dz=7)

    def stripe(dz, flip):
        core = 1 - c if flip else c
        row = pl.multiple_of(32 * lax.rem(z + dz, 8) + 16 * core, 16)
        return pltpu.make_async_remote_copy(
            src_ref=raw.at[:, pl.ds(row, 16), :],
            dst_ref=qw[0].at[:, 0, (8 - dz) % 8, 0, 0, c],
            send_sem=stripe_send.at[dz, flip],
            recv_sem=stripe_recv.at[dz, c],
            device_id=place.device(dz=dz, other=bool(flip)),
            device_id_type=MESH,
        )

    def stripe_arrival(dz, core):
        return pltpu.make_async_remote_copy(
            src_ref=raw.at[:, pl.ds(0, 16), :],
            dst_ref=qw[0].at[:, 0, (8 - dz) % 8, 0, 0, core],
            send_sem=stripe_send.at[dz, core],
            recv_sem=stripe_recv.at[dz, core],
            device_id=other,
            device_id_type=MESH,
        )

    swap = net.make(raw, pw.at[0, xh], place.swap())
    own_row = pl.multiple_of(32 * z + 16 * c, 16)
    other_row = pl.multiple_of(32 * z + 16 * (1 - c), 16)

    @pl.when(c != xh)
    def _():
        swap.start()

    for dz in ZS:
        for flip in range(2):
            stripe(dz, flip).start()
    stripe(0, 1).start()
    qw[0][:, 0, 0, 0, 0, c] = raw[:, pl.ds(own_row, 16), :]

    ups, downs, beside = {}, {}, {}

    def forward(step, ri):
        up, down = (8 - step) % 8, step
        if step < 3 or (step == 3 and ri == 0):
            ups[step, ri] = net.make(pw.at[up, c, ri], pw.at[up - 1 if up else 7, c, ri], plus)
        if step < 3 or (step == 3 and ri == 1):
            downs[step, ri] = net.make(pw.at[down, c, ri], pw.at[down + 1, c, ri], minus)
        return [group[step, ri] for group in (ups, downs) if (step, ri) in group]

    def share(rel, ri):
        beside[rel, ri] = net.make(pw.at[rel, c, ri], pw.at[rel, c, ri], other)
        return [beside[rel, ri]]

    def launch(copies, keep=True):
        for copy in copies:
            copy.start()
        if keep:
            net.open.extend(copies)

    first = []
    for ri in range(2):
        first += forward(0, ri)
    for ri in range(2):
        first += share(0, ri)
    net.open.extend(first)

    @pl.when(straight)
    def _():
        pw[0, c] = raw[...]
        launch(first, False)

    prepare()
    give_left = net.make(lp.at[1], lp.at[0], other)
    give_right = net.make(rown.at[1], rown.at[0], other)

    @pl.when(straight)
    def _():
        for i in range(3):
            rown[0, i] = rt[i, pl.ds(own_row, 16), :]
            rown[1, i] = rt[i, pl.ds(other_row, 16), :]
        give_right.start()
        give_left.start()
        lp[0] = lp[1]

    @pl.when(c != xh)
    def _():
        swap.wait_recv()
        launch(first, False)
        give_right.wait_recv()

    rq[:, 0, 0, xh] = rown[0]
    for dz in (0, 1, 7, 2, 6, 3, 5, 4):
        for core in range(2):
            if dz:
                stripe_arrival(dz, core).wait_recv()
    stripe_arrival(0, 1 - c).wait_recv()

    turned_x = (0, xl, 1, 1 - xl)

    def tile(h, px, py):
        return qw[py // 2].at[h, turned_x[px], :, py % 2, px % 2]

    def sent_tile(h, px, py, dx, dy):
        qx, qy = (px + 4 - dx) % 4, (py + 4 - dy) % 4
        there = lax.rem(xl + dx, 2)
        turned = (0, there, 1, 1 - there)[qx]
        return qw[qy // 2].at[h, turned, :, qy % 2, qx % 2]

    def pass_on(h, px, py, dx, dy):
        return net.start(tile(h, px, py), sent_tile(h, px, py, dx, dy), place.device(dx=dx, dy=dy))

    rows, columns, factor, rest, early, late = {}, {}, {}, [], [], []
    for d in (2, 1, 3):
        rows[d] = pass_on(0, 0, 0, d, 0)
        columns[d] = pass_on(1, 0, 0, 0, d)
    for d in (2, 1, 3):
        factor[d] = net.start(rq.at[:, 0, 0, xh], rq.at[:, 4 - d, 0, xh], place.device(dy=d))
    for d in (2, 1, 3):
        rest.append(pass_on(1, 0, 0, d, 0))
        rest.append(pass_on(0, 0, 0, 0, d))

    def ring(step):
        for ri in range(2):
            if step < 4:
                ups[step - 1, ri].wait_recv()
                downs[step - 1, ri].wait_recv()
                launch(forward(step, ri) + share(8 - step, ri) + share(step, ri))
            else:
                (ups if ri == 0 else downs)[3, ri].wait_recv()
                launch(share(4, ri))

    ring(1)
    meanwhile()
    for d in (1, 3, 2):
        factor[d].wait_recv()
    for dx in (2, 1, 3):
        early.append(
            net.start(
                rq.at[:, :, 0, xh], rq.at[:, :, (4 - dx) % 2, xh], place.device(dx=dx)
            )
        )
    for d in (1, 3, 2):
        rows[d].wait_recv()
        early.append(pass_on(0, 4 - d, 0, 0, 3))
        late.append(pass_on(0, 4 - d, 0, 0, 1))
    columns[3].wait_recv()
    for dx in (2, 1, 3):
        early.append(pass_on(1, 0, 1, dx, 0))
    for d in (1, 3, 2):
        late.append(pass_on(0, 4 - d, 0, 0, 2))
        if d != 3:
            columns[d].wait_recv()
            for dx in (2, 1, 3):
                late.append(pass_on(1, 0, 4 - d, dx, 0))
    ring(2)
    ring(3)
    ring(4)
    for copy in rest + early:
        copy.wait_recv()

    @pl.when(c != xh)
    def _():
        give_left.wait_recv()

    turn_columns()
    for copy in beside.values():
        copy.wait_recv()
    turn_rows()
    for copy in late:
        copy.wait_recv()

    @pl.when(c != xh)
    def _():
        swap.wait_send()

    @pl.when(straight)
    def _():
        give_right.wait_send()
        give_left.wait_send()

    for dz in ZS:
        for flip in range(2):
            stripe(dz, flip).wait_send()
    stripe(0, 1).wait_send()


def dot(a, b, ca, cb):
    return lax.dot_general(a, b, (((ca,), (cb,)), ((), ())), preferred_element_type=F32)


def form_screen(half, rq, lp, screen):
    lane = lax.broadcasted_iota(jnp.int32, (256, 128), 1)
    columns = slice(half * 128, half * 128 + 128)
    for i in range(3):
        factor = rq[i, 2 * half : 2 * half + 2].reshape(128, 128)
        rows = lp[0, i]
        zero = jnp.zeros_like(rows)
        screen[2 * i, :, columns] = dot(jnp.where(lane < 64, rows, zero), factor, 1, 1)
        screen[2 * i + 1, :, columns] = dot(jnp.where(lane < 64, zero, rows), factor, 1, 1)


def seat(z, word):
    w = lax.div(word, 64)
    return lax.div(w, 8), lax.rem(lax.rem(w, 8) - z + 8, 8)


def form_rows(z, code, pw, wide, xp, xpt):
    for k in range(NK):
        u, rel = seat(z, code[k])
        raw = jnp.concatenate([pw[rel, u, 0], pw[rel, u, 1]], axis=1)
        turned = dot(raw, wide[k], 1, 0).astype(BF)
        xp[k] = turned
        xpt[k] = jnp.concatenate([turned[:, :128], turned[:, 128:]], axis=0).T


def form_columns(half, place, code, qw, wide, xq):
    for k in range(NK):
        u, rel = seat(place.z, code[k])
        turned = jnp.where(u == place.xh, 0, 1)
        raw = jnp.concatenate(
            [
                qw[half][0, turned, rel].reshape(128, 128),
                qw[half][1, turned, rel].reshape(128, 128),
            ],
            axis=1,
        )
        xq[k, half * 128 : half * 128 + 128] = dot(raw, wide[k], 1, 0).astype(BF)


def form_density(half, xp, xq, density):
    columns = slice(half * 128, half * 128 + 128)
    for k in range(NK):
        rows = xp[k]
        stacked = jnp.concatenate(
            [rows, jnp.concatenate([rows[:, 128:], -rows[:, :128]], axis=1)], axis=0
        )
        density[k, :, columns] = dot(stacked, xq[k, columns], 1, 1)


def mix(half, ks, screen, density, mixed):
    columns = pl.ds(half * 128, 128)

    def step(t, carry):
        top = pl.multiple_of(t * 16, 16)
        s = [screen[i, pl.ds(top, 16), columns] for i in range(STOPS)]
        for part in range(2):
            source = pl.multiple_of(part * 256 + top, 16)
            d = [density[j, pl.ds(source, 16), columns] for j in range(NK)]
            for k in ks:
                total = d[(k + 3) % NK] * s[0]
                for i in range(1, STOPS):
                    total = total + d[(k + 3 - i) % NK] * s[i]
                mixed[k, pl.ds(top, 16), pl.ds(part * 256 + half * 128, 128)] = total.astype(BF)
        return carry

    lax.fori_loop(0, 16, step, 0, unroll=4)


def close(ks, xpt, xq, mixed, e):
    ys = []
    for k in ks:
        q = xq[k]
        operand = jnp.concatenate(
            [q, jnp.concatenate([-q[:, 128:], q[:, :128]], axis=1)], axis=0
        )
        ys.append(dot(mixed[k], operand, 1, 0).astype(BF))
    for k, y in zip(ks, ys):
        turned = jnp.concatenate([y, jnp.concatenate([y[:, 128:], -y[:, :128]], axis=1)], axis=0)
        e[k] = dot(xpt[k], turned, 1, 0).reshape(8, 2, 8, 256)


def close_and_reduce(place, net, screen, density, xpt, xq, mixed, e, sib, sb, rb, sz, zb, out):
    c, x, y, z, xh, xl = place.c, place.x, place.y, place.z, place.xh, place.xl
    other = place.device(other=True)

    def batch(b):
        return [8 * h + b * SIZE + i for h in range(2) for i in range(SIZE)]

    def hand(first):
        ks = pl.ds(first, SIZE)
        return net.start(e.at[ks, :, 1 - c], sib.at[ks], other)

    def fold(b, copies):
        for h in range(2):
            copies[h].wait_recv()
            for i in range(b * SIZE, (b + 1) * SIZE):
                value = e[8 * h + i, :, c] + sib[8 * h + i]
                value = jnp.concatenate([value[:, :, :128], value[:, :, 128:]], axis=1)
                sb[h, :, i] = value.astype(BF)

    def scatter(b):
        copies = []
        zz = pl.ds(b * SIZE, SIZE)
        for dx, dy in FAR_FIRST:
            tx = lax.rem(x + dx, 4)
            ty = lax.rem(y + dy, 4)
            copies.append(
                net.start(
                    sb.at[lax.div(tx, 2), ty * 2 + lax.rem(tx, 2), zz],
                    rb.at[dx * 4 + dy, zz],
                    place.device(dx=dx, dy=dy),
                )
            )
        return copies

    def collect(b, copies):
        zz = pl.ds(b * SIZE, SIZE)
        total = sb[xh, y * 2 + xl, zz].astype(F32)
        for (dx, dy), copy in zip(reversed(FAR_FIRST), reversed(copies)):
            copy.wait_recv()
            total = total + rb[dx * 4 + dy, zz].astype(F32)
        sz[zz] = total.astype(BF)

    handed, sent = {}, {}
    for b in range(BATCHES):
        ks = batch(b)
        mix(1, ks, screen, density, mixed)
        if b:
            fold(b - 1, handed[b - 1])
            sent[b - 1] = scatter(b - 1)
        handed[b] = []
        for h in range(2):
            close(ks[h * SIZE : h * SIZE + SIZE], xpt, xq, mixed, e)
            handed[b].append(hand(8 * h + b * SIZE))
    fold(BATCHES - 1, handed[BATCHES - 1])
    sent[BATCHES - 1] = scatter(BATCHES - 1)
    for b in range(BATCHES):
        collect(b, sent[b])
    last = []
    for dz in ZS:
        last.append(net.start(sz.at[lax.rem(z + dz, 8)], zb.at[dz], place.device(dz=dz)))
    value = sz[z].astype(F32)
    for dz, copy in zip(ZS, last):
        copy.wait_recv()
        value = value + zb[dz].astype(F32)
    value = value * (1.0 / (4.0 * NPTS * math.sqrt(NB)))
    out[0, 0] = value[:8]
    out[1, 0] = value[8:]


FAR_FIRST = tuple(sorted(PLANE, key=lambda d: -min(d[0], 4 - d[0]) - min(d[1], 4 - d[1])))
BATCHES = 2
SIZE = 8 // BATCHES


def kernel(
    star, star_op, wedge, rotations, screen_left, screen_right, out,
    tables, ops, left, right, raw, pw, qw_near, qw_far, rq, lp, rt, rown, code, turns, wide, xp, xpt, xq, screen,
    density, mixed, e, sib, sb, rb, sz, zb, send, recv, stripe_send, stripe_recv, local,
):
    place = Place()
    net = Copies(send, recv)
    qw = (qw_near, qw_far)
    fetches = [
        pltpu.make_async_copy(source, target, local.at[i])
        for i, (source, target) in enumerate(
            (
                (wedge.at[:, 0], raw),
                (screen_right, right),
                (screen_left, left),
                (star, tables),
                (star_op, ops),
                (rotations, turns),
            )
        )
    ]
    for fetch in fetches:
        fetch.start()
    barrier = pltpu.get_barrier_semaphore()
    peers = [place.device(other=True)]
    peers += [place.device(dz=d, other=flip) for d in range(1, 8) for flip in (False, True)]
    peers += [place.device(dx=d) for d in (1, 2, 3)] + [place.device(dy=d) for d in (1, 2, 3)]
    greet(barrier, peers)

    @pl.when(place.c != place.xh)
    def _():
        greet(barrier, [place.swap()])

    fetches[0].wait()

    @pl.when(place.c != place.xh)
    def _():
        pl.semaphore_wait(barrier, len(peers) + 1)

    @pl.when(place.c == place.xh)
    def _():
        pl.semaphore_wait(barrier, len(peers))

    def prepare():
        fetches[1].wait()
        fetches[2].wait()
        factors(left, right, lp, rt)

    def meanwhile():
        for fetch in fetches[3:]:
            fetch.wait()
        decode(tables, ops, code)
        widen(code, turns, wide)

    def turn_columns():
        form_screen(0, rq, lp, screen)
        form_columns(0, place, code, qw, wide, xq)

    def turn_rows():
        form_rows(place.z, code, pw, wide, xp, xpt)
        form_density(0, xp, xq, density)
        mix(0, range(NK), screen, density, mixed)

    gather(
        place, net, raw, pw, qw, rq, lp, rt, rown, stripe_send, stripe_recv,
        prepare, meanwhile, turn_columns, turn_rows,
    )
    form_screen(1, rq, lp, screen)
    form_columns(1, place, code, qw, wide, xq)
    form_density(1, xp, xq, density)
    close_and_reduce(place, net, screen, density, xpt, xq, mixed, e, sib, sb, rb, sz, zb, out)
    net.finish()


VM = pl.BlockSpec(memory_space=pltpu.VMEM)
HB = pl.BlockSpec(memory_space=pl.ANY)
COPIES = 180


def body(wedge_orbitals, star_members, star_ops, rotations, screen_left, screen_right):
    sem = pltpu.SemaphoreType.DMA((COPIES,))
    return pl.pallas_call(
        kernel,
        out_shape=jax.ShapeDtypeStruct((2, 1, 8, 128), F32),
        in_specs=[HB] * 6,
        out_specs=VM,
        scratch_shapes=[
            pltpu.SMEM((4, NK), jnp.int32),
            pltpu.SMEM((4, NK), jnp.int32),
            pltpu.VMEM((STOPS, 64, 256), BF),
            pltpu.VMEM((STOPS, 64, 256), BF),
            pltpu.VMEM((2, 256, NB), BF),
            pltpu.VMEM((8, 2, 2, 256, 128), BF),
            pltpu.VMEM((2, 2, 8, 2, 2, 2, 16, 128), BF),
            pltpu.VMEM((2, 2, 8, 2, 2, 2, 16, 128), BF),
            pltpu.VMEM((3, 4, 2, 2, 16, 128), BF),
            pltpu.VMEM((2, 3, 256, 128), BF),
            pltpu.VMEM((3, 256, 128), BF),
            pltpu.VMEM((2, 3, 16, 128), BF),
            pltpu.SMEM((NK,), jnp.int32),
            pltpu.VMEM((48, NB, NB), BF),
            pltpu.VMEM((NK, 256, 256), BF),
            pltpu.VMEM((NK, 256, 256), BF),
            pltpu.VMEM((NK, NB, 512), BF),
            pltpu.VMEM((NK, 256, 256), BF),
            pltpu.VMEM((STOPS, 256, 256), F32),
            pltpu.VMEM((NK, 512, 256), F32),
            pltpu.VMEM((NK, 256, 512), BF),
            pltpu.VMEM((NK, 8, 2, 8, 256), F32),
            pltpu.VMEM((NK, 8, 8, 256), F32),
            pltpu.VMEM((2, 8, 8, 16, 128), BF),
            pltpu.VMEM((16, 8, 16, 128), BF),
            pltpu.VMEM((8, 16, 128), BF),
            pltpu.VMEM((8, 16, 128), BF),
            sem,
            sem,
            pltpu.SemaphoreType.DMA((8, 2)),
            pltpu.SemaphoreType.DMA((8, 2)),
            pltpu.SemaphoreType.DMA((6,)),
        ],
        compiler_params=pltpu.CompilerParams(
            collective_id=0, has_side_effects=True, vmem_limit_bytes=56 << 20
        ),
    )(
        star_members.T,
        star_ops.T,
        wedge_orbitals,
        rotations,
        jnp.swapaxes(screen_left, 1, 2),
        jnp.swapaxes(screen_right, 1, 2),
    )


def solution(mesh):
    return jax.shard_map(
        body,
        mesh=mesh,
        in_specs=(
            P(None, "ka", "pt", None),
            P(),
            P(),
            P(),
            P(None, "pt", None),
            P(None, "pt", None),
        ),
        out_specs=P(None, "ka", "pt", None),
        check_vma=False,
    )
```
